32 devices in a mesh: expert: 4 (over y, x), dp: 8 (over z, core).
Axes of the slice: x: 2, y: 2, z: 4, core: 2. Of those that a mesh axis runs over, the one named last changes fastest.
Arguments:
- tokens_in: bfloat16 [16384, 768], P(('expert', 'dp')), may hold values from -6 to 6
- segment_ids: int32 [32, 512], P(('expert', 'dp')), may hold values from 0 to 7, never falling along the last dimension, each value on 1 to 256 neighbouring positions
- expert_index: int32 [16384], P(('expert', 'dp')), may hold values from 0 to 3, as said below
- expert_slot: int32 [16384], P(('expert', 'dp')), may hold values from 0 to 191, as said below
- attn_gain: bfloat16 [2, 768], P(None, ('expert', 'dp')), may hold values from 0.099609375 to 1.8984375
- qkv_weight: bfloat16 [768, 2, 2304], P(('expert', 'dp')), may hold values from -0.21875 to 0.21875
- out_weight: bfloat16 [768, 2, 768], P(('expert', 'dp')), may hold values from -1.75 to 1.75
- rel_bias: float32 [32, 12], replicated, may hold values from -4 to 4
- ffn_gain: bfloat16 [2, 768], P(None, ('expert', 'dp')), may hold values from 0.099609375 to 1.8984375
- ffn_in: bfloat16 [768, 3072], P(('expert', 'dp')), may hold values from -0.21875 to 0.21875
- ffn_out: bfloat16 [3072, 768], P(('expert', 'dp')), may hold values from -0.109375 to 0.109375
- router: bfloat16 [768, 4], P(('expert', 'dp')), may hold values from -0.14941406 to 0.14941406
- expert_in: bfloat16 [4, 768, 3072], P('expert', 'dp'), may hold values from -0.21875 to 0.21875
- expert_out: bfloat16 [4, 3072, 768], P('expert', 'dp'), may hold values from -0.875 to 0.875
- cotangent: bfloat16 [16384, 768], P(('expert', 'dp')), may hold values from -6 to 6
Outputs:
- tokens_out: bfloat16 [16384, 768], P(('expert', 'dp'))
- tokens_grad: float32 [16384, 768], P(('expert', 'dp'))
- attn_gain_grad: float32 [2, 768], P(None, ('expert', 'dp'))
- qkv_weight_grad: float32 [768, 2, 2304], P(('expert', 'dp'))
- out_weight_grad: float32 [768, 2, 768], P(('expert', 'dp'))
- rel_bias_grad: float32 [32, 12], replicated
- ffn_gain_grad: float32 [2, 768], P(None, ('expert', 'dp'))
- ffn_in_grad: float32 [768, 3072], P(('expert', 'dp'))
- ffn_out_grad: float32 [3072, 768], P(('expert', 'dp'))
- router_grad: float32 [768, 4], P(('expert', 'dp'))
- expert_in_grad: float32 [4, 768, 3072], P('expert', 'dp')
- expert_out_grad: float32 [4, 3072, 768], P('expert', 'dp')
The draws below stay inside these ranges and needn't reach their ends.
Inputs may be any that keep to these rules, and one draw needn't show every extreme that they name: `expert_index`: in every draw one expert is named by 128 + 64 tokens of every device; every other expert by at most 128 tokens of one device. `expert_slot`: the tokens of one device that name one expert hold distinct slots; a slot of 128 or more drops the token. The busiest expert's tokens of every device hold the slots 0 to 191; the others' slots are below 128.
All inputs are finite; a program needn't handle non-finite values.
Results may differ from the reference program's by a relative error of at most 0.024.
Values may be sent and summed in bfloat16 or wider, within the bound.
No kernel may reach another device: no remote copies, remote signals or barrier semaphores. Data moves between devices by JAX's collectives and lax.ppermute only.
A program may use at most 256 MiB of HBM per device.

```python
import math
import jax
import jax.numpy as jnp
import numpy as np
from jax import lax

D = 768
HEADS = 12
DH = 64
FF = 3072
BUCKETS = 32
SEQ = 512
LAYERS = 2
EXPERTS = 4
TOK_DEV = 512
SEQS = 32
TOKENS = 16384
CAP = 128
DROP = 64


def route_table(key):
    busy_expert = jax.random.randint(jax.random.fold_in(key, 101), (), 0, EXPERTS)
    block_keys = jax.random.split(jax.random.fold_in(key, 102), TOKENS // TOK_DEV)

    def one_block(block_key):
        first_key, second_key, third_key = jax.random.split(block_key, 3)
        others = jax.random.permutation(first_key, (EXPERTS - 1) * CAP)[:TOK_DEV - CAP - DROP]
        other_experts = others // CAP
        other_experts = other_experts + (other_experts >= busy_expert).astype(jnp.int32)
        busy_slots = jax.random.permutation(second_key, CAP + DROP)
        experts_all = jnp.concatenate([jnp.full((CAP + DROP,), busy_expert, jnp.int32), other_experts.astype(jnp.int32)])
        slots_all = jnp.concatenate([busy_slots.astype(jnp.int32), (others % CAP).astype(jnp.int32)])
        token_order = jax.random.permutation(third_key, TOK_DEV)
        return (experts_all[token_order], slots_all[token_order])
    expert_ids, slot_ids = jax.vmap(one_block)(block_keys)
    return (expert_ids.reshape(-1), slot_ids.reshape(-1))


def draw_expert_index(key, part):
    routes = route_table(key)
    return routes[0]


def draw_expert_slot(key, part):
    routes = route_table(key)
    return routes[1]


def spiked(values, key, source, target, shards_of, factor):
    def block_of(dim):
        return (jnp.arange(values.shape[dim]) // (values.shape[dim] // shards_of)).reshape((-1,) + (1,) * (values.ndim - 1 - dim))

    one_side = jax.random.permutation(key, shards_of)[block_of(target)]
    second = (block_of(target) + shards_of // 2) % shards_of
    return jnp.where((block_of(source) == one_side) | (block_of(source) == second), factor * values, values)


def levels(key, shape, cuts, smallest, largest):
    def one(axis_at, parts):
        steps = jax.random.uniform(jax.random.fold_in(jax.random.fold_in(key, 6), axis_at), (parts,), jnp.float32, smallest / len(cuts), largest / len(cuts))
        return jnp.repeat(jnp.exp(steps), shape[axis_at] // parts).reshape((-1,) + (1,) * (len(shape) - axis_at - 1))

    level = one(*cuts[0])
    for cut in cuts[1:]:
        level = level * one(*cut)
    return level


def split_up(count, total, reach, skew):
    weights = [(1 << 20) // math.isqrt(grade ** skew) + 1 for grade in range(2, count + 1)]
    rest, given = total - reach - (count - 1), [1] * (count - 1)
    while rest > 0:
        candidates = [i for i in range(count - 1) if given[i] < reach]
        whole, left = sum([weights[i] for i in candidates]), rest
        for i in candidates:
            addition = min(reach - given[i], max(1, left * weights[i] // whole), rest)
            given[i] = given[i] + addition
            rest = rest - addition
    return np.array([reach] + given)


def uneven(key, amount, total, bound, slope):
    if amount == 2:
        one = jax.random.randint(key, (), max(1, total - bound), min(bound, total - 1) + 1)
        return jnp.stack([one, total - one])
    lengths = jnp.asarray(split_up(amount, total, bound, slope), jnp.int32)
    couples = (amount - 1) // 2
    giver, receiver = lengths[1:1 + 2 * couples:2], lengths[2:2 + 2 * couples:2]
    margin = jnp.minimum(giver - 1, bound - receiver)
    shifted = jax.random.randint(jax.random.fold_in(key, 1), (couples,), 0, 1 << 20) % (margin + 1)
    lengths = lengths.at[1:1 + 2 * couples:2].set(giver - shifted).at[2:2 + 2 * couples:2].set(receiver + shifted)
    return lengths[jax.random.permutation(jax.random.fold_in(key, 2), amount)]


def centred(stream_key, shape, spread, most, cuts=(), held_as=jnp.bfloat16):
    drawn = spread * jax.random.normal(stream_key, shape, jnp.float32)
    if cuts:
        drawn = drawn * levels(stream_key, shape, cuts, -0.22, 0.18)
    return jnp.clip(drawn, -most, most).astype(held_as)


def noise_with(stream_key, extent, scale, reach, pieces, heavy, held_as=jnp.bfloat16):
    drawn = scale * jax.random.normal(stream_key, extent, jnp.float32)
    if pieces:
        drawn = drawn * levels(stream_key, extent, pieces, -0.22, 0.18)
    return jnp.clip(spiked(drawn, jax.random.fold_in(stream_key, 3), *heavy), -reach, reach).astype(held_as)


def setup_inputs(seed: int = 0) -> dict:
    splits = jax.random.split(jax.random.key(seed), 16)
    tokens_in = noise_with(splits[0], (TOKENS, D), 1.0, 6.0, ((0, 32),), (0, 1, 32, 2.75))
    segment_ids = jax.vmap(lambda own: jnp.searchsorted(jnp.cumsum(uneven(own, 8, SEQ, SEQ // 2, 0)), jnp.arange(SEQ), side="right"))(jax.random.split(splits[1], SEQS)).reshape((SEQS, SEQ)).astype(jnp.int32)
    expert_index = draw_expert_index(jax.random.fold_in(splits[15], 71), 0)
    expert_slot = draw_expert_slot(jax.random.fold_in(splits[15], 71), 0)
    attn_gain = jnp.clip(1.0 + 0.18 * jax.random.normal(splits[4], (LAYERS, D), jnp.float32), 0.099609375, 1.8984375).astype(jnp.bfloat16)
    qkv_weight = centred(splits[5], (D, LAYERS, 3 * D), D ** -0.5, 0.21875, ((0, 32),))
    out_weight = centred(splits[6], (D, LAYERS, D), (D // 64) ** -0.5, 1.75, ((0, 32),))
    rel_bias = centred(splits[7], (BUCKETS, HEADS), 1.0, 4.0, (), jnp.float32)
    ffn_gain = jnp.clip(1.0 + 0.18 * jax.random.normal(splits[8], (LAYERS, D), jnp.float32), 0.099609375, 1.8984375).astype(jnp.bfloat16)
    ffn_in = centred(splits[9], (D, FF), D ** -0.5, 0.21875, ((0, 32),))
    ffn_out = centred(splits[10], (FF, D), FF ** -0.5, 0.109375, ((0, 32),))
    router = centred(splits[11], (D, EXPERTS), 0.02, 0.14941406, ((0, 32),))
    expert_in = centred(splits[12], (EXPERTS, D, FF), D ** -0.5, 0.21875, ((0, 4), (1, 8)))
    expert_out = centred(splits[13], (EXPERTS, FF, D), (max(1, FF // (4 * EXPERTS * EXPERTS))) ** -0.5, 0.875, ((0, 4), (1, 8)))
    cotangent = centred(splits[14], (TOKENS, D), 1.0, 6.0, ((0, 32),))
    return {"tokens_in": tokens_in, "segment_ids": segment_ids, "expert_index": expert_index, "expert_slot": expert_slot, "attn_gain": attn_gain, "qkv_weight": qkv_weight, "out_weight": out_weight, "rel_bias": rel_bias, "ffn_gain": ffn_gain, "ffn_in": ffn_in, "ffn_out": ffn_out, "router": router, "expert_in": expert_in, "expert_out": expert_out, "cotangent": cotangent}


EPSILON = 1e-06
NEG_FILL = -1e+30
PRECISE = lax.Precision.HIGHEST

@jax.custom_vjp
def low(v):
    return lax.optimization_barrier(v.astype(jnp.bfloat16)).astype(jnp.float32)

@jax.custom_vjp
def low_back(v):
    return v

def low_keep(v):
    return (low(v), None)

def low_pass(kept, grad):
    return (grad,)

def back_keep(v):
    return (v, None)

def back_low(kept, grad):
    return (low(grad),)
low.defvjp(low_keep, low_pass)
low_back.defvjp(back_keep, back_low)

def both_ways(value):
    return low(low_back(value))

def bucket_of(offset):
    distance = jnp.abs(offset)
    far_bucket = jnp.full_like(distance, 8)
    for level_id in range(1, 8):
        far_bucket = far_bucket + (distance * distance >= 64 * 2 ** level_id).astype(jnp.int32)
    near_bucket = jnp.where(distance < 8, distance, far_bucket)
    return near_bucket + 16 * (offset > 0).astype(jnp.int32)

def offset_onehot():
    offsets = jnp.arange(2 * SEQ - 1, dtype=jnp.int32) - (SEQ - 1)
    return (bucket_of(offsets)[:, None] == jnp.arange(BUCKETS, dtype=jnp.int32)[None, :]).astype(jnp.float32)

def norm_scale(stream, gain_row):
    inverse = lax.rsqrt(lax.optimization_barrier(jnp.mean(stream * stream, axis=-1, keepdims=True)) + EPSILON)
    return stream * inverse * gain_row

def gelu_tanh(value):
    return jax.nn.gelu(value, approximate=True)

def attend(packed, segments, offset_bias):
    seq_count = segments.shape[0]
    grouped = packed.reshape(seq_count, SEQ, 3, HEADS, DH)
    positions = jnp.arange(SEQ, dtype=jnp.int32)[None, :] - jnp.arange(SEQ, dtype=jnp.int32)[:, None] + SEQ - 1
    bias_full = jnp.take(offset_bias, positions, axis=1)

    def one_sequence(entry):
        rows_qkv, seg_row = entry
        raw_scores = low_back(jnp.einsum('qhd,khd->hqk', rows_qkv[:, 0], rows_qkv[:, 1], precision=PRECISE))
        allowed = (seg_row[:, None] == seg_row[None, :])[None]
        scores = jnp.where(allowed, raw_scores * DH ** (-0.5) + bias_full, NEG_FILL)
        weights_now = low(jax.nn.softmax(scores, axis=-1))
        mixed_rows = both_ways(jnp.einsum('hqk,khd->qhd', weights_now, rows_qkv[:, 2], precision=PRECISE))
        return mixed_rows.reshape(SEQ, HEADS * DH)
    return lax.map(jax.checkpoint(one_sequence), (grouped, segments)).reshape(-1, HEADS * DH)

def sparse_branch(normed, router_full, in_full, out_experts, expert_index, expert_slot):
    logits = low_back(jnp.dot(normed, router_full, precision=PRECISE))
    chosen = (expert_index[:, None] == jnp.arange(EXPERTS, dtype=jnp.int32)[None, :]).astype(jnp.float32)
    gate_values = lax.optimization_barrier(jnp.sum(jax.nn.softmax(logits, axis=-1) * chosen, axis=-1))
    block_count = normed.shape[0] // TOK_DEV
    target = jnp.where(expert_slot < CAP, expert_index * CAP + expert_slot, -1).reshape(block_count, TOK_DEV)
    slot_table = (target[:, :, None] == jnp.arange(EXPERTS * CAP, dtype=jnp.int32)[None, None, :]).astype(jnp.float32)
    grouped = normed.reshape(block_count, TOK_DEV, -1)
    buffers = jnp.einsum('bts,btd->bsd', slot_table, grouped, precision=PRECISE)
    buffers = low_back(buffers.reshape(block_count, EXPERTS, CAP, -1))
    hidden = low_back(jnp.einsum('becd,edf->becf', buffers, in_full, precision=PRECISE))
    hidden = both_ways(gelu_tanh(hidden))
    produced = both_ways(jnp.einsum('becf,efd->becd', hidden, out_experts, precision=PRECISE))
    combined = jnp.einsum('bts,bsd->btd', slot_table, produced.reshape(block_count, EXPERTS * CAP, -1), precision=PRECISE)
    return gate_values[:, None] * combined.reshape(normed.shape)

def layers(source, gains_attn, qkv_full, out_full, bias_table, gains_ffn, ffn_in_full, ffn_out_full, router_full, in_full, out_experts, segment_ids, expert_index, expert_slot):
    offset_bias = jnp.dot(offset_onehot(), bias_table, precision=PRECISE).T
    stream = source
    for layer_id in range(2):
        normed = low(norm_scale(stream, gains_attn[layer_id]))
        packed = both_ways(jnp.dot(normed, qkv_full[:, layer_id], precision=PRECISE))
        mixed = attend(packed, segment_ids, offset_bias)
        stream = stream + low_back(jnp.dot(mixed, out_full[:, layer_id], precision=PRECISE))
        normed = low(norm_scale(stream, gains_ffn[layer_id]))
        if layer_id == 0:
            hidden = low_back(jnp.dot(normed, ffn_in_full, precision=PRECISE))
            hidden = both_ways(gelu_tanh(hidden))
            stream = stream + low_back(jnp.dot(hidden, ffn_out_full, precision=PRECISE))
        else:
            stream = stream + sparse_branch(normed, router_full, in_full, out_experts, expert_index, expert_slot)
    return stream

def reference(tokens_in, segment_ids, expert_index, expert_slot, attn_gain, qkv_weight, out_weight, rel_bias, ffn_gain, ffn_in, ffn_out, router, expert_in, expert_out, cotangent):

    def forward(source, gains_attn, qkv_full, out_full, bias_table, gains_ffn, ffn_in_full, ffn_out_full, router_full, in_full, out_experts):
        return layers(source, gains_attn, qkv_full, out_full, bias_table, gains_ffn, ffn_in_full, ffn_out_full, router_full, in_full, out_experts, segment_ids, expert_index, expert_slot)
    result, pull_back = jax.vjp(forward, tokens_in.astype(jnp.float32), attn_gain.astype(jnp.float32), qkv_weight.astype(jnp.float32), out_weight.astype(jnp.float32), rel_bias.astype(jnp.float32), ffn_gain.astype(jnp.float32), ffn_in.astype(jnp.float32), ffn_out.astype(jnp.float32), router.astype(jnp.float32), expert_in.astype(jnp.float32), expert_out.astype(jnp.float32))
    gradients = pull_back(cotangent.astype(jnp.float32))
    return (result.astype(jnp.bfloat16), gradients[0], gradients[1], gradients[2], gradients[3], gradients[4], gradients[5], gradients[6], gradients[7], gradients[8], gradients[9], gradients[10])
```

```python
import functools
import math

import jax
import jax.numpy as jnp
from jax import lax
from jax.experimental import pallas as pl
from jax.experimental.pallas import tpu as pltpu
from jax.sharding import Mesh, PartitionSpec as P

HEADS = 12
DH = 64
BUCKETS = 32
SEQ = 512


EPSILON = 1e-06
NEG_FILL = -1e30
PRECISE = lax.Precision.HIGHEST


def bucket_of(offset):
    distance = jnp.abs(offset)
    far_bucket = jnp.full_like(distance, 8)
    for level_id in range(1, 8):
        far_bucket = far_bucket + (distance * distance >= 64 * 2**level_id).astype(jnp.int32)
    near_bucket = jnp.where(distance < 8, distance, far_bucket)
    return near_bucket + 16 * (offset > 0).astype(jnp.int32)


def norm_scale(stream, gain_row):
    inverse = lax.rsqrt(jnp.mean(stream * stream, axis=-1, keepdims=True) + EPSILON)
    return stream * inverse * gain_row


def norm_backward(grad_normed, stream, gain_row):
    normed_again, norm_pull = jax.vjp(norm_scale, stream, gain_row.astype(jnp.float32))
    grad_input, grad_gain = norm_pull(grad_normed)
    return (grad_input, grad_gain)


def gelu_tanh(value):
    return jax.nn.gelu(value, approximate=True)


def gate_of(logits, chosen):
    return jnp.sum(jax.nn.softmax(logits, axis=-1) * chosen, axis=-1)


EXPERT_AXES = ("ey", "ex")
DATA_AXES = ("z", "core")
ALL_AXES = ("ey", "ex", "z", "core")
SPAN = 2 * SEQ
ROWS = 128
VMEM_BYTES = 48 * 1024 * 1024
BF16 = jnp.bfloat16
F32 = jnp.float32
ATTEND_COST = 22 * 10**9


def swap_with(value, axes, count, flip):
    return lax.ppermute(value, axes, [(i, i ^ flip) for i in range(count)])


def place_kernel(count, axis, cuts, me_ref, *refs):
    sources = refs[:count]
    targets = refs[count : count + len(cuts)]
    held, in_sems, out_sems = refs[count + len(cuts) :]
    arriving = [
        pltpu.make_async_copy(sources[flip], held.at[flip], in_sems.at[flip]) for flip in range(count)
    ]
    for copy in arriving:
        copy.start()
    leaving = []
    for flip in range(count):
        slot = me_ref[0] ^ flip
        arriving[flip].wait()
        for cut_id, group in enumerate(cuts):
            target = targets[cut_id]
            target = target.at[slot] if axis == 0 else target.at[:, slot]
            for part_id, (first, last) in enumerate(group):
                origin = held.at[flip]
                if axis == 1:
                    origin = origin.at[:, :, first:last]
                spot = target if len(group) == 1 else target.at[:, part_id]
                copy = pltpu.make_async_copy(origin, spot, out_sems.at[flip, cut_id, part_id])
                copy.start()
                leaving.append(copy)
    for copy in leaving:
        copy.wait()


def place(parts, me, axis=0, cuts=None):
    shape = parts[0].shape
    groups = cuts or (((0, shape[-1]),),)
    outs = []
    for group in groups:
        own = shape[:-1] + (group[0][1] - group[0][0],)
        lead = own[:axis] + (len(parts),) + ((len(group),) if len(group) > 1 else ())
        outs.append(jax.ShapeDtypeStruct(lead + own[axis:], parts[0].dtype))
    moved = sum(math.prod(o.shape) for o in outs) * 4
    most = max(len(group) for group in groups)
    placed = pl.pallas_call(
        functools.partial(place_kernel, len(parts), axis, groups),
        out_shape=outs,
        in_specs=[pl.BlockSpec(memory_space=pltpu.SMEM)]
        + [pl.BlockSpec(memory_space=pl.ANY)] * len(parts),
        out_specs=[pl.BlockSpec(memory_space=pl.ANY)] * len(outs),
        scratch_shapes=[
            pltpu.VMEM((len(parts),) + shape, parts[0].dtype),
            pltpu.SemaphoreType.DMA((len(parts),)),
            pltpu.SemaphoreType.DMA((len(parts), len(groups), most)),
        ],
        compiler_params=pltpu.CompilerParams(vmem_limit_bytes=VMEM_BYTES),
        cost_estimate=pl.CostEstimate(flops=0, bytes_accessed=2 * moved, transcendentals=0),
    )(me.astype(jnp.int32).reshape(1), *parts)
    return placed if cuts else placed[0]


def together(*values):
    return lax.optimization_barrier(values)


def gather_z(shard):
    depth = lax.axis_size("z")
    along = [shard] + [swap_with(shard, "z", depth, k) for k in range(1, depth)]
    return place(along, lax.axis_index("z"))


def gather_across(line):
    experts = lax.axis_size(EXPERT_AXES)
    across = [line] + [swap_with(line, EXPERT_AXES, experts, k) for k in range(1, experts)]
    half = place(across, lax.axis_index(EXPERT_AXES))
    return half.reshape((-1,) + line.shape[1:])


def gather_core(half, cuts):
    other = swap_with(half, "core", 2, 1)
    whole = place([half, other], lax.axis_index("core"), axis=1, cuts=cuts)
    return [part.reshape(-1, part.shape[-1]) for part in whole]


def tree_sum(terms):
    while len(terms) > 1:
        terms = [terms[i] + terms[i + 1] for i in range(0, len(terms), 2)]
    return terms[0]


def scatter_stage(pieces, axes, axis):
    count = lax.axis_size(axes)
    me = lax.axis_index(axes)

    def of(slot):
        own = [lax.dynamic_index_in_dim(p, slot, axis, keepdims=False) for p in pieces]
        return own[0] if len(own) == 1 else jnp.concatenate(own, axis=-1)

    terms = [of(me)]
    for flip in range(1, count):
        terms.append(swap_with(of(me ^ flip), axes, count, flip))
    return tree_sum([t.astype(F32) for t in terms])


def scatter_core(grads):
    groups = lax.axis_size(EXPERT_AXES) * lax.axis_size("z")
    pieces = []
    for grad, blocks in grads:
        rows = grad.shape[0] // (2 * groups * blocks)
        split = grad.reshape(groups, 2, blocks, rows, grad.shape[-1])
        pieces.extend(split[:, :, block] for block in range(blocks))
    return scatter_stage(pieces, "core", 1).astype(BF16)


def scatter_across(half):
    experts = lax.axis_size(EXPERT_AXES)
    return scatter_stage([half.reshape((experts, -1) + half.shape[1:])], EXPERT_AXES, 0).astype(BF16)


def scatter_z(line):
    return scatter_stage([line], "z", 0)


def sum_everywhere(value):
    for axes in ("core", EXPERT_AXES, "z"):
        count = lax.axis_size(axes)
        value = tree_sum([value] + [swap_with(value, axes, count, k) for k in range(1, count)])
    return value


def bias_kernel(row_ref, seg_col_ref, seg_row_ref, out_ref):
    offsets = jnp.broadcast_to(row_ref[0], (ROWS, SPAN))
    seg_row = seg_row_ref[...]
    for first in range(0, SEQ, ROWS):
        turned = pltpu.roll(offsets, first, 1, stride=1, stride_axis=0)[:, :SEQ]
        same = seg_col_ref[first : first + ROWS, :] == seg_row
        out_ref[0, first : first + ROWS, :] = jnp.where(same, turned, NEG_FILL)


def offset_onehot():
    columns = jnp.arange(SPAN, dtype=jnp.int32)
    offsets = jnp.where(columns < SEQ, columns, columns - SPAN)
    return (bucket_of(offsets)[:, None] == jnp.arange(BUCKETS, dtype=jnp.int32)[None, :]).astype(F32)


def masked_bias(rel_bias, segments):
    by_offset = jnp.dot(offset_onehot(), rel_bias, precision=PRECISE).T
    return pl.pallas_call(
        bias_kernel,
        grid=(HEADS,),
        in_specs=[
            pl.BlockSpec((1, 1, SPAN), lambda h: (h, 0, 0)),
            pl.BlockSpec((SEQ, 1), lambda h: (0, 0)),
            pl.BlockSpec((1, SEQ), lambda h: (0, 0)),
        ],
        out_specs=pl.BlockSpec((1, SEQ, SEQ), lambda h: (h, 0, 0)),
        out_shape=jax.ShapeDtypeStruct((HEADS, SEQ, SEQ), F32),
        compiler_params=pltpu.CompilerParams(vmem_limit_bytes=VMEM_BYTES),
        cost_estimate=pl.CostEstimate(flops=ATTEND_COST // 3, bytes_accessed=HEADS * SEQ * SEQ * 8, transcendentals=0),
    )(by_offset.reshape(HEADS, 1, SPAN), segments.reshape(SEQ, 1), segments.reshape(1, SEQ))


def dot_nt(a, b):
    return lax.dot_general(a, b, (((1,), (1,)), ((), ())), preferred_element_type=F32)


def dot_tn(a, b):
    return lax.dot_general(a, b, (((0,), (0,)), ((), ())), preferred_element_type=F32)


def half_masks(rows):
    lanes = lax.broadcasted_iota(jnp.int32, (rows, 2 * DH), 1)
    return (lanes < DH, lanes >= DH)


def attend_kernel(q_ref, k_ref, v_ref, bias_ref, mixed_ref, prob_ref):
    keys = k_ref[...]
    values = v_ref[...]
    masks = half_masks(ROWS)
    for first in range(0, SEQ, ROWS):
        rows = slice(first, first + ROWS)
        query = q_ref[rows, :] * BF16(DH ** (-0.5))
        mixed = []
        for head in range(2):
            own = jnp.where(masks[head], query, jnp.zeros_like(query))
            scores = dot_nt(own, keys) + bias_ref[head, rows, :]
            grown = jnp.exp(scores - jnp.max(scores, axis=-1, keepdims=True))
            prob = (grown * (1.0 / jnp.sum(grown, axis=-1, keepdims=True))).astype(BF16)
            prob_ref[head, rows, :] = prob
            mixed.append(jnp.dot(prob, values, preferred_element_type=F32))
        mixed_ref[rows, :] = jnp.where(masks[0], mixed[0], mixed[1]).astype(BF16)


PAIRS = HEADS // 2


def attend_forward(packed, bias):
    def columns(base):
        return pl.BlockSpec((SEQ, 2 * DH), lambda p: (0, base + p))

    return pl.pallas_call(
        attend_kernel,
        grid=(PAIRS,),
        in_specs=[
            columns(0),
            columns(PAIRS),
            columns(2 * PAIRS),
            pl.BlockSpec((2, SEQ, SEQ), lambda p: (p, 0, 0)),
        ],
        out_specs=[columns(0), pl.BlockSpec((2, SEQ, SEQ), lambda p: (p, 0, 0))],
        out_shape=[
            jax.ShapeDtypeStruct((SEQ, HEADS * DH), BF16),
            jax.ShapeDtypeStruct((HEADS, SEQ, SEQ), BF16),
        ],
        compiler_params=pltpu.CompilerParams(vmem_limit_bytes=VMEM_BYTES),
        cost_estimate=pl.CostEstimate(
            flops=ATTEND_COST,
            bytes_accessed=HEADS * SEQ * SEQ * 6,
            transcendentals=HEADS * SEQ * SEQ,
        ),
    )(packed, packed, packed, bias)


def attend_back_kernel(q_ref, k_ref, v_ref, grad_ref, prob_ref, out_ref, diag_ref, raw_ref, shift_ref):
    pair = pl.program_id(0)
    keys = k_ref[...]
    values = v_ref[...]
    query = q_ref[...]
    grads = grad_ref[...]
    masks = half_masks(ROWS)
    full_mask = half_masks(SEQ)[0]
    grad_query = [[None] * (SEQ // ROWS) for head in range(2)]
    grad_key = []
    grad_value = []
    for head in range(2):
        shift_ref[...] = jnp.zeros_like(shift_ref)
        for block in range(SEQ // ROWS):
            rows = slice(block * ROWS, (block + 1) * ROWS)
            grad_rows = grad_ref[rows, :]
            own = jnp.where(masks[head], grad_rows, jnp.zeros_like(grad_rows))
            grad_prob = dot_nt(own, values)
            prob = prob_ref[head, rows, :].astype(F32)
            weighted = prob * grad_prob
            grad_scores = weighted - prob * jnp.sum(weighted, axis=-1, keepdims=True)
            start = SEQ - ROWS * (block + 1)
            shift_ref[:, start : start + SEQ] += grad_scores
            raw = (grad_scores * DH ** (-0.5)).astype(BF16)
            raw_ref[rows, :] = raw
            grad_query[head][block] = jnp.dot(raw, keys, preferred_element_type=F32)
        grad_key.append(dot_tn(raw_ref[...], query))
        grad_value.append(dot_tn(prob_ref[head], grads))
        total = shift_ref[0:8, :]
        for group in range(1, ROWS // 8):
            total = total + pltpu.roll(
                shift_ref[8 * group : 8 * group + 8, :], SPAN - 8 * group, 1
            )
        diag_ref[0, head] = total
    width = 2 * DH

    def put(base, rows, value):
        spot = pl.multiple_of((base + pair) * width, width)
        out_ref[rows, pl.ds(spot, width)] = value.astype(BF16)

    for block in range(SEQ // ROWS):
        rows = slice(block * ROWS, (block + 1) * ROWS)
        put(0, rows, jnp.where(masks[0], grad_query[0][block], grad_query[1][block]))
    everything = slice(0, SEQ)
    put(PAIRS, everything, jnp.where(full_mask, grad_key[0], grad_key[1]))
    put(2 * PAIRS, everything, jnp.where(full_mask, grad_value[0], grad_value[1]))


def attend_backward(packed, grad_mixed, prob):
    def columns(base):
        return pl.BlockSpec((SEQ, 2 * DH), lambda p: (0, base + p))

    width = 3 * HEADS * DH
    return pl.pallas_call(
        attend_back_kernel,
        grid=(PAIRS,),
        in_specs=[
            columns(0),
            columns(PAIRS),
            columns(2 * PAIRS),
            columns(0),
            pl.BlockSpec((2, SEQ, SEQ), lambda p: (p, 0, 0)),
        ],
        out_specs=[
            pl.BlockSpec((SEQ, width), lambda p: (0, 0)),
            pl.BlockSpec((1, 2, 8, SPAN), lambda p: (p, 0, 0, 0)),
        ],
        out_shape=[
            jax.ShapeDtypeStruct((SEQ, width), BF16),
            jax.ShapeDtypeStruct((PAIRS, 2, 8, SPAN), F32),
        ],
        scratch_shapes=[pltpu.VMEM((SEQ, SEQ), BF16), pltpu.VMEM((ROWS, SPAN), F32)],
        compiler_params=pltpu.CompilerParams(vmem_limit_bytes=VMEM_BYTES),
        cost_estimate=pl.CostEstimate(
            flops=ATTEND_COST,
            bytes_accessed=HEADS * SEQ * SEQ * 2 + SEQ * width * 4,
            transcendentals=0,
        ),
    )(packed, packed, packed, grad_mixed, prob)


def bias_grad(diagonals):
    columns = jnp.arange(SPAN, dtype=jnp.int32)[None, :]
    offsets = columns - jnp.arange(8, dtype=jnp.int32)[:, None] - (SEQ - ROWS)
    offsets = jnp.where(offsets >= SEQ, offsets - SPAN, offsets)
    table = (bucket_of(offsets)[:, :, None] == jnp.arange(BUCKETS, dtype=jnp.int32)).astype(F32)
    return jnp.einsum(
        "hs,sb->bh",
        diagonals.reshape(HEADS, 8 * SPAN),
        table.reshape(8 * SPAN, BUCKETS),
        precision=PRECISE,
    )


def attention_forward(stream, gain_row, qkv_full, out_full, bias):
    normed_low = norm_scale(stream, gain_row.astype(F32)).astype(BF16)
    packed_low = jnp.dot(normed_low, qkv_full, preferred_element_type=F32).astype(BF16)
    mixed_low, prob_low = attend_forward(packed_low, bias)
    stream_after = stream + jnp.dot(mixed_low, out_full, preferred_element_type=F32)
    return (normed_low, packed_low, mixed_low, prob_low, stream_after)


def attention_back_in(grad_stream, out_full, kept_state):
    grad_low = grad_stream.astype(BF16)
    grad_out_w = jnp.einsum("td,te->de", kept_state[2], grad_low, preferred_element_type=F32)
    grad_mixed = jnp.einsum("te,de->td", grad_low, out_full, preferred_element_type=F32)
    return (grad_mixed.astype(BF16), grad_out_w.astype(BF16))


def attention_back_out(packed_grad, grad_stream, stream, gain_row, qkv_full, kept_state):
    grad_normed = jnp.einsum("te,de->td", packed_grad, qkv_full, preferred_element_type=F32)
    grad_input, grad_gain = norm_backward(grad_normed, stream, gain_row)
    return (grad_stream + grad_input, grad_gain)


def qkv_weight_term(packed_grad, kept_state):
    return jnp.einsum("td,te->de", kept_state[0], packed_grad, preferred_element_type=F32).astype(BF16)


def dense_forward(stream, gain_row, weight_in, weight_out):
    normed_low = norm_scale(stream, gain_row.astype(jnp.float32)).astype(jnp.bfloat16)
    hidden_pre = jnp.dot(normed_low, weight_in, preferred_element_type=jnp.float32)
    hidden_low = gelu_tanh(hidden_pre).astype(jnp.bfloat16)
    stream_after = stream + jnp.dot(hidden_low, weight_out, preferred_element_type=jnp.float32)
    return (normed_low, hidden_pre, stream_after)


def dense_back_in(grad_stream, weight_out, kept_state):
    grad_low = grad_stream.astype(jnp.bfloat16)
    gelu_value, gelu_pull = jax.vjp(gelu_tanh, kept_state[1])
    hidden_low = gelu_value.astype(jnp.bfloat16)
    grad_hidden = (
        jnp.einsum("td,fd->tf", grad_low, weight_out, preferred_element_type=jnp.float32)
        .astype(jnp.bfloat16)
        .astype(jnp.float32)
    )
    grad_pre = gelu_pull(grad_hidden)[0].astype(jnp.bfloat16)
    return (hidden_low, grad_low, grad_pre)


def dense_back_out(
    grad_stream, stream, gain_row, weight_in, hidden_low, grad_low, grad_pre, kept_state
):
    grad_w_out = jnp.einsum("tf,td->fd", hidden_low, grad_low, preferred_element_type=jnp.float32)
    grad_w_in = jnp.einsum("td,tf->df", kept_state[0], grad_pre, preferred_element_type=jnp.float32)
    grad_normed = jnp.einsum("tf,df->td", grad_pre, weight_in, preferred_element_type=jnp.float32)
    grad_input, grad_gain = norm_backward(grad_normed, stream, gain_row)
    return (
        grad_stream + grad_input,
        grad_gain,
        grad_w_in.astype(jnp.bfloat16),
        grad_w_out.astype(jnp.bfloat16),
    )


def dispatch_table(expert_ids, slot_ids, expert_count, capacity):
    target = jnp.where(slot_ids < capacity, expert_ids * capacity + slot_ids, -1)
    return (
        target[:, None] == jnp.arange(expert_count * capacity, dtype=jnp.int32)[None, :]
    ).astype(jnp.bfloat16)


def expert_forward(received, weight_in, weight_out):
    hidden_pre = jnp.einsum(
        "secd,edf->secf", received, weight_in, preferred_element_type=jnp.float32
    )
    hidden_low = gelu_tanh(hidden_pre).astype(jnp.bfloat16)
    produced = jnp.einsum(
        "secf,efd->secd", hidden_low, weight_out, preferred_element_type=jnp.float32
    )
    return (produced.astype(jnp.bfloat16), hidden_pre, received)


def sparse_forward(
    stream, gain_row, router_full, in_full, out_experts, expert_ids, slot_ids, expert_count
):
    normed_low = norm_scale(stream, gain_row.astype(jnp.float32)).astype(jnp.bfloat16)
    logits = jnp.dot(normed_low, router_full, preferred_element_type=jnp.float32)
    chosen = (expert_ids[:, None] == jnp.arange(expert_count, dtype=jnp.int32)[None, :]).astype(
        jnp.float32
    )
    gate_values = gate_of(logits, chosen)
    capacity = stream.shape[0] // expert_count
    slot_table = dispatch_table(expert_ids, slot_ids, expert_count, capacity)
    outgoing = jnp.einsum(
        "ts,td->sd", slot_table, normed_low, preferred_element_type=jnp.float32
    ).astype(jnp.bfloat16)
    outgoing = outgoing.reshape(expert_count // in_full.shape[0], in_full.shape[0], capacity, -1)
    produced, hidden_pre, received = expert_forward(
        lax.all_to_all(outgoing, EXPERT_AXES, split_axis=0, concat_axis=0, tiled=True),
        in_full,
        out_experts,
    )
    returned = lax.all_to_all(produced, EXPERT_AXES, split_axis=0, concat_axis=0, tiled=True)
    combined = jnp.dot(
        slot_table,
        returned.reshape(expert_count * capacity, -1),
        preferred_element_type=jnp.float32,
    )
    stream_after = stream + gate_values[:, None] * combined
    return (
        (normed_low, logits, chosen, gate_values, slot_table, combined, hidden_pre, received),
        stream_after,
    )


def sparse_backward(grad_stream, stream, gain_row, router_full, in_full, out_experts, kept_state):
    normed_low, logits, chosen, gate_values, slot_table, combined, hidden_pre, received = kept_state
    grad_gates = jnp.sum(grad_stream * combined, axis=-1)
    grad_combined = (gate_values[:, None] * grad_stream).astype(jnp.bfloat16)
    outgoing = jnp.einsum(
        "ts,td->sd", slot_table, grad_combined, preferred_element_type=jnp.float32
    ).astype(jnp.bfloat16)
    grad_produced = lax.all_to_all(
        outgoing.reshape(received.shape), EXPERT_AXES, split_axis=0, concat_axis=0, tiled=True
    )
    gelu_value, gelu_pull = jax.vjp(gelu_tanh, hidden_pre)
    hidden_low = gelu_value.astype(jnp.bfloat16)
    grad_w_out = jnp.einsum(
        "secf,secd->efd", hidden_low, grad_produced, preferred_element_type=jnp.float32
    )
    grad_hidden = (
        jnp.einsum("secd,efd->secf", grad_produced, out_experts, preferred_element_type=jnp.float32)
        .astype(jnp.bfloat16)
        .astype(jnp.float32)
    )
    grad_pre = gelu_pull(grad_hidden)[0].astype(jnp.bfloat16)
    grad_w_in = jnp.einsum("secd,secf->edf", received, grad_pre, preferred_element_type=jnp.float32)
    grad_received = jnp.einsum(
        "secf,edf->secd", grad_pre, in_full, preferred_element_type=jnp.float32
    ).astype(jnp.bfloat16)
    grad_sent = lax.all_to_all(grad_received, EXPERT_AXES, split_axis=0, concat_axis=0, tiled=True)
    grad_normed = jnp.dot(
        slot_table, grad_sent.reshape(slot_table.shape[1], -1), preferred_element_type=jnp.float32
    )
    gate_again, gate_pull = jax.vjp(gate_of, logits, chosen)
    grad_logits = gate_pull(grad_gates)[0].astype(jnp.bfloat16)
    grad_router = jnp.einsum(
        "td,te->de", normed_low, grad_logits, preferred_element_type=jnp.float32
    )
    grad_normed = grad_normed + jnp.einsum(
        "te,de->td", grad_logits, router_full, preferred_element_type=jnp.float32
    )
    grad_input, grad_gain = norm_backward(grad_normed, stream, gain_row)
    return (grad_stream + grad_input, grad_gain, grad_router, grad_w_in, grad_w_out)


def on_device(
    tokens_in,
    segment_ids,
    expert_index,
    expert_slot,
    attn_gain,
    qkv_weight,
    out_weight,
    rel_bias,
    ffn_gain,
    ffn_in,
    ffn_out,
    router,
    expert_in,
    expert_out,
    cotangent,
):
    width = tokens_in.shape[1]
    packed_width = qkv_weight.shape[2]
    expert_count = router.shape[1]
    small = jnp.concatenate([attn_gain.T, ffn_gain.T, router], axis=1)
    small_width = -(-small.shape[1] // 128) * 128
    small = jnp.pad(small, ((0, 0), (0, small_width - small.shape[1])))
    joined = packed_width + width
    hidden_width = ffn_in.shape[1]
    rows = ffn_in.shape[0]
    stack = ffn_out.shape[0] // rows
    first_shard = jnp.concatenate([qkv_weight[:, 0], out_weight[:, 0], small], axis=1)
    last_shard = jnp.concatenate([qkv_weight[:, 1], out_weight[:, 1]], axis=1)
    dense_shard = jnp.concatenate(
        [ffn_in] + [ffn_out[i * rows : (i + 1) * rows] for i in range(stack)], axis=1
    )
    first_line = gather_z(first_shard)
    first_line, dense_shard, last_shard, expert_in, expert_out = together(
        first_line, dense_shard, last_shard, expert_in, expert_out
    )
    in_full = lax.all_gather(expert_in, DATA_AXES, axis=1, tiled=True)
    out_experts = lax.all_gather(expert_out, DATA_AXES, axis=1, tiled=True)
    first_half = gather_across(first_line)
    dense_line = gather_z(dense_shard)
    first_half, dense_line = together(first_half, dense_line)
    qkv_zero, out_zero, small_full = gather_core(
        first_half,
        (((0, packed_width),), ((packed_width, joined),), ((joined, joined + small_width),)),
    )
    last_line = gather_z(last_shard)
    dense_half = gather_across(dense_line)
    dense_half, last_line = together(dense_half, last_line)
    ffn_in_full, ffn_out_full = gather_core(
        dense_half,
        (
            ((0, hidden_width),),
            tuple((hidden_width + i * width, hidden_width + (i + 1) * width) for i in range(stack)),
        ),
    )
    last_half = gather_across(last_line)
    qkv_one, out_one = gather_core(last_half, (((0, packed_width),), ((packed_width, joined),)))
    gains = small_full[:, :4].T
    router_full = small_full[:, 4 : 4 + expert_count]
    bias = masked_bias(rel_bias, segment_ids)

    stream_zero = tokens_in.astype(F32)
    attn_zero = attention_forward(stream_zero, gains[0], qkv_zero, out_zero, bias)
    dense_zero = dense_forward(attn_zero[4], gains[2], ffn_in_full, ffn_out_full)
    attn_one = attention_forward(dense_zero[2], gains[1], qkv_one, out_one, bias)
    sparse_one, stream_two = sparse_forward(
        attn_one[4],
        gains[3],
        router_full,
        in_full,
        out_experts,
        expert_index,
        expert_slot,
        expert_count,
    )

    grad_top = cotangent.astype(F32)
    grad_middle, ffn_gain_one, router_term, expert_in_term, expert_out_term = sparse_backward(
        grad_top, attn_one[4], gains[3], router_full, in_full, out_experts, sparse_one
    )
    expert_out_sum = lax.psum_scatter(
        expert_out_term.astype(BF16), DATA_AXES, scatter_dimension=1, tiled=True
    ).astype(F32)
    expert_in_sum = lax.psum_scatter(
        expert_in_term.astype(BF16), DATA_AXES, scatter_dimension=1, tiled=True
    ).astype(F32)

    grad_mixed_one, out_one_term = attention_back_in(grad_middle, out_one, attn_one)
    packed_grad_one, pairs_one = attend_backward(attn_one[1], grad_mixed_one, attn_one[3])
    qkv_one_term = qkv_weight_term(packed_grad_one, attn_one)
    grad_one, attn_gain_one = attention_back_out(
        packed_grad_one, grad_middle, dense_zero[2], gains[1], qkv_one, attn_one
    )
    last_half = scatter_core([(qkv_one_term, 1), (out_one_term, 1)])

    hidden_low, grad_low, grad_pre = dense_back_in(grad_one, ffn_out_full, dense_zero)
    last_half, grad_pre = together(last_half, grad_pre)
    last_line = scatter_across(last_half)
    grad_half, ffn_gain_zero, ffn_in_term, ffn_out_term = dense_back_out(
        grad_one, attn_zero[4], gains[2], ffn_in_full, hidden_low, grad_low, grad_pre, dense_zero
    )
    dense_half = scatter_core([(ffn_in_term, 1), (ffn_out_term, stack)])
    grad_mixed_zero, out_zero_term = attention_back_in(grad_half, out_zero, attn_zero)
    dense_half, grad_mixed_zero = together(dense_half, grad_mixed_zero)
    dense_line = scatter_across(dense_half)
    packed_grad_zero, pairs_zero = attend_backward(attn_zero[1], grad_mixed_zero, attn_zero[3])
    last_line, packed_grad_zero = together(last_line, packed_grad_zero)
    one_sum = scatter_z(last_line)
    qkv_zero_term = qkv_weight_term(packed_grad_zero, attn_zero)
    first_half = scatter_core([(qkv_zero_term, 1), (out_zero_term, 1)])
    grad_zero, attn_gain_zero = attention_back_out(
        packed_grad_zero, grad_half, stream_zero, gains[0], qkv_zero, attn_zero
    )
    first_half, grad_zero, dense_line = together(first_half, grad_zero, dense_line)
    first_line = scatter_across(first_half)
    dense_sum = scatter_z(dense_line)
    zero_sum = scatter_z(first_line)
    ffn_in_sum = dense_sum[:, :hidden_width]
    ffn_out_sum = jnp.concatenate(
        [dense_sum[:, hidden_width + i * width : hidden_width + (i + 1) * width] for i in range(stack)]
    )
    qkv_sum = jnp.stack([zero_sum[:, :packed_width], one_sum[:, :packed_width]], axis=1)
    out_sum = jnp.stack([zero_sum[:, packed_width:], one_sum[:, packed_width:]], axis=1)

    bias_term = bias_grad(pairs_zero + pairs_one)
    tiny = jnp.concatenate(
        [
            attn_gain_zero,
            attn_gain_one,
            ffn_gain_zero,
            ffn_gain_one,
            router_term.reshape(-1),
            bias_term.reshape(-1),
        ]
    )
    tiny_sum = sum_everywhere(tiny.reshape(-1, 128)).reshape(-1)
    gain_sums = tiny_sum[: 4 * width].reshape(4, width)
    router_sums = tiny_sum[4 * width : (4 + expert_count) * width].reshape(width, expert_count)
    bias_sum = tiny_sum[(4 + expert_count) * width :].reshape(BUCKETS, HEADS)
    first_row = lax.axis_index(ALL_AXES) * rows
    gain_shard = lax.dynamic_slice_in_dim(gain_sums, first_row, rows, 1)
    router_shard = lax.dynamic_slice_in_dim(router_sums, first_row, rows, 0)
    return (
        stream_two.astype(BF16),
        grad_zero,
        gain_shard[:2],
        qkv_sum,
        out_sum,
        bias_sum,
        gain_shard[2:],
        ffn_in_sum,
        ffn_out_sum,
        router_shard,
        expert_in_sum,
        expert_out_sum,
    )


def solution(mesh):
    experts, data = mesh.shape["expert"], mesh.shape["dp"]
    side = 1 << ((experts.bit_length() - 1) // 2)
    fine = Mesh(mesh.devices.reshape(experts // side, side, data // 2, 2), ALL_AXES)
    placed = (
        P(ALL_AXES, None),
        P(ALL_AXES, None),
        P(ALL_AXES),
        P(ALL_AXES),
        P(None, ALL_AXES),
        P(ALL_AXES, None, None),
        P(ALL_AXES, None, None),
        P(),
        P(None, ALL_AXES),
        P(ALL_AXES, None),
        P(ALL_AXES, None),
        P(ALL_AXES, None),
        P(EXPERT_AXES, DATA_AXES, None),
        P(EXPERT_AXES, DATA_AXES, None),
        P(ALL_AXES, None),
    )
    return jax.shard_map(
        on_device,
        mesh=fine,
        in_specs=placed,
        out_specs=(
            P(ALL_AXES, None),
            P(ALL_AXES, None),
            P(None, ALL_AXES),
            P(ALL_AXES, None, None),
            P(ALL_AXES, None, None),
            P(),
            P(None, ALL_AXES),
            P(ALL_AXES, None),
            P(ALL_AXES, None),
            P(ALL_AXES, None),
            P(EXPERT_AXES, DATA_AXES, None),
            P(EXPERT_AXES, DATA_AXES, None),
        ),
        check_vma=False,
    )
```

```python
import functools
import math

import jax
import jax.numpy as jnp
from jax import lax
from jax.experimental import pallas as pl
from jax.experimental.pallas import tpu as pltpu
from jax.sharding import Mesh, PartitionSpec as P

HEADS = 12
DH = 64
BUCKETS = 32
SEQ = 512


EPSILON = 1e-06
NEG_FILL = -1e30
PRECISE = lax.Precision.HIGHEST


def bucket_of(offset):
    distance = jnp.abs(offset)
    far_bucket = jnp.full_like(distance, 8)
    for level_id in range(1, 8):
        far_bucket = far_bucket + (distance * distance >= 64 * 2**level_id).astype(jnp.int32)
    near_bucket = jnp.where(distance < 8, distance, far_bucket)
    return near_bucket + 16 * (offset > 0).astype(jnp.int32)


def norm_scale(stream, gain_row):
    inverse = lax.rsqrt(jnp.mean(stream * stream, axis=-1, keepdims=True) + EPSILON)
    return stream * inverse * gain_row


def norm_backward(grad_normed, stream, gain_row):
    normed_again, norm_pull = jax.vjp(norm_scale, stream, gain_row.astype(jnp.float32))
    grad_input, grad_gain = norm_pull(grad_normed)
    return (grad_input, grad_gain)


def gelu_tanh(value):
    return jax.nn.gelu(value, approximate=True)


def gate_of(logits, chosen):
    return jnp.sum(jax.nn.softmax(logits, axis=-1) * chosen, axis=-1)


EXPERT_AXES = ("ey", "ex")
DATA_AXES = ("z", "core")
ALL_AXES = ("ey", "ex", "z", "core")
SPAN = 2 * SEQ
ROWS = 128
CHUNK = 256
VMEM_BYTES = 24 * 1024 * 1024
BF16 = jnp.bfloat16
F32 = jnp.float32
ATTEND_COST = HEADS * SEQ * SEQ


def swap_with(value, axes, count, flip):
    return lax.ppermute(value, axes, [(i, i ^ flip) for i in range(count)])


def place_kernel(count, pieces, axis, cuts, me_ref, *refs):
    sources = refs[: len(pieces)]
    targets = refs[len(pieces) : len(pieces) + len(cuts)]
    held, in_sems, out_sems = refs[len(pieces) + len(cuts) :]
    arriving = [[] for flip in range(count)]
    for source_id, (flip, first, rows) in enumerate(pieces):
        spot = held.at[flip]
        if rows:
            spot = spot.at[first : first + rows]
        copy = pltpu.make_async_copy(sources[source_id], spot, in_sems.at[source_id])
        copy.start()
        arriving[flip].append(copy)
    leaving = []
    for flip in range(count):
        slot = me_ref[0] ^ flip
        for copy in arriving[flip]:
            copy.wait()
        for cut_id, group in enumerate(cuts):
            target = targets[cut_id]
            target = target.at[slot] if axis == 0 else target.at[:, slot]
            for part_id, (first, last) in enumerate(group):
                origin = held.at[flip]
                if axis == 1:
                    origin = origin.at[:, :, first:last]
                elif len(cuts) > 1:
                    origin = origin.at[:, first:last]
                spot = target if len(group) == 1 else target.at[:, part_id]
                copy = pltpu.make_async_copy(origin, spot, out_sems.at[flip, cut_id, part_id])
                copy.start()
                leaving.append(copy)
    for copy in leaving:
        copy.wait()


def room_for(elements, rows):
    return elements // rows * (-(-rows // 16) * 16) * 2 + (1 << 20)


def place(parts, me, axis=0, cuts=None):
    sources, pieces = [], []
    for flip, part in enumerate(parts):
        first = 0
        for piece in part if isinstance(part, list) else [part]:
            pieces.append((flip, first, piece.shape[0] if isinstance(part, list) else 0))
            sources.append(piece)
            first += piece.shape[0]
    shape = parts[0].shape
    groups = cuts or (((0, shape[-1]),),)
    outs = []
    for group in groups:
        own = shape[:-1] + (group[0][1] - group[0][0],)
        lead = own[:axis] + (len(parts),) + ((len(group),) if len(group) > 1 else ())
        outs.append(jax.ShapeDtypeStruct(lead + own[axis:], parts[0].dtype))
    moved = sum(math.prod(o.shape) for o in outs) * 4
    most = max(len(group) for group in groups)
    placed = pl.pallas_call(
        functools.partial(place_kernel, len(parts), tuple(pieces), axis, groups),
        out_shape=outs,
        in_specs=[pl.BlockSpec(memory_space=pltpu.SMEM)]
        + [pl.BlockSpec(memory_space=pl.ANY)] * len(sources),
        out_specs=[pl.BlockSpec(memory_space=pl.ANY)] * len(outs),
        scratch_shapes=[
            pltpu.VMEM((len(parts),) + shape, parts[0].dtype),
            pltpu.SemaphoreType.DMA((len(sources),)),
            pltpu.SemaphoreType.DMA((len(parts), len(groups), most)),
        ],
        compiler_params=pltpu.CompilerParams(
            vmem_limit_bytes=room_for(math.prod(shape) * len(parts), shape[-2])
        ),
        cost_estimate=pl.CostEstimate(flops=0, bytes_accessed=2 * moved, transcendentals=0),
    )(me.astype(jnp.int32).reshape(1), *sources)
    return placed if cuts else placed[0]


def together(*values):
    return lax.optimization_barrier(values)


def after(value, *earlier):
    return lax.optimization_barrier((value,) + earlier)[0]


def send_z(shard, *earlier):
    depth = lax.axis_size("z")
    along = [shard] + [swap_with(shard, "z", depth, k) for k in range(1, depth - 1)]
    last = after(shard, *earlier) if earlier else shard
    return along + [swap_with(last, "z", depth, depth - 1)]


def gather_z(along, cuts=None):
    return place(along, lax.axis_index("z"), cuts=cuts)


def send_across(line):
    experts = lax.axis_size(EXPERT_AXES)
    return [line] + [swap_with(line, EXPERT_AXES, experts, k) for k in range(1, experts)]


def send_around(line, *earlier):
    if lax.axis_size("ey") != 2 or lax.axis_size("ex") != 2:
        return send_across(line)
    near_x = swap_with(line, "ex", 2, 1)
    near_y = swap_with(line, "ey", 2, 1)
    middle = line.shape[0] // 2
    from_x, from_y = together(near_x, near_y, *earlier)[:2]
    far = [
        swap_with(from_x[:middle], "ey", 2, 1),
        swap_with(from_y[middle:], "ex", 2, 1),
    ]
    return [line, near_x, near_y, far]


def gather_across(across, *earlier):
    if earlier:
        across = [across[0], after(across[1], *earlier)] + across[2:]
    half = place(across, lax.axis_index(EXPERT_AXES))
    return half.reshape((-1,) + half.shape[2:])


def gather_core(half, cuts, *earlier):
    other = swap_with(half, "core", 2, 1)
    if earlier:
        other = after(other, *earlier)
    whole = place([half, other], lax.axis_index("core"), axis=1, cuts=cuts)
    return [part.reshape(-1, part.shape[-1]) for part in whole]


def tree_sum(terms):
    while len(terms) > 1:
        terms = [terms[i] + terms[i + 1] for i in range(0, len(terms), 2)]
    return terms[0]


def exchange(whole, axes):
    return lax.all_to_all(whole, axes, split_axis=0, concat_axis=0, tiled=True)


def sum_z(line):
    depth = lax.axis_size("z")
    me = lax.axis_index("z")
    terms = [lax.dynamic_index_in_dim(line, me, 0, keepdims=False)]
    for flip in range(1, depth):
        block = lax.dynamic_index_in_dim(line, me ^ flip, 0, keepdims=False)
        terms.append(swap_with(block, "z", depth, flip))
    return tree_sum([t.astype(F32) for t in terms])


def sum_terms(terms, *earlier):
    if earlier:
        terms = after(terms, *earlier)
    return jnp.sum(terms.astype(F32), axis=0)


def split_kernel(widths, me_ref, *refs):
    count = len(widths)
    sources = refs[:count]
    targets = refs[count : count + 2]
    held, in_sems, out_sems = refs[count + 2 :]
    arriving = []
    for flip in range(2):
        slot = me_ref[0] ^ flip
        first = 0
        for part_id, width in enumerate(widths):
            spot = held.at[flip]
            if count > 1:
                spot = spot.at[:, :, first : first + width]
            copy = pltpu.make_async_copy(sources[part_id].at[:, slot], spot, in_sems.at[flip, part_id])
            copy.start()
            arriving.append(copy)
            first += width
    leaving = []
    for flip in range(2):
        for copy in arriving[flip * count : (flip + 1) * count]:
            copy.wait()
        copy = pltpu.make_async_copy(held.at[flip], targets[flip], out_sems.at[flip])
        copy.start()
        leaving.append(copy)
    for copy in leaving:
        copy.wait()


def scatter_core(grads, *earlier):
    groups = lax.axis_size(EXPERT_AXES) * lax.axis_size("z")
    pieces = [g.reshape(groups, 2, g.shape[0] // (2 * groups), g.shape[1]) for g in grads]
    widths = tuple(g.shape[1] for g in grads)
    out = jax.ShapeDtypeStruct((groups, pieces[0].shape[2], sum(widths)), BF16)
    kept, sent = pl.pallas_call(
        functools.partial(split_kernel, widths),
        out_shape=[out, out],
        in_specs=[pl.BlockSpec(memory_space=pltpu.SMEM)]
        + [pl.BlockSpec(memory_space=pl.ANY)] * len(pieces),
        out_specs=[pl.BlockSpec(memory_space=pl.ANY)] * 2,
        scratch_shapes=[
            pltpu.VMEM((2,) + out.shape, BF16),
            pltpu.SemaphoreType.DMA((2, len(pieces))),
            pltpu.SemaphoreType.DMA((2,)),
        ],
        compiler_params=pltpu.CompilerParams(
            vmem_limit_bytes=room_for(2 * math.prod(out.shape), out.shape[-2])
        ),
        cost_estimate=pl.CostEstimate(
            flops=0, bytes_accessed=8 * math.prod(out.shape), transcendentals=0
        ),
    )(lax.axis_index("core").astype(jnp.int32).reshape(1), *pieces)
    other = swap_with(sent, "core", 2, 1)
    if earlier:
        other = after(other, *earlier)
    return (kept.astype(F32) + other.astype(F32)).astype(BF16)


def send_half(half):
    experts = lax.axis_size(EXPERT_AXES)
    return exchange(half.reshape((experts, -1) + half.shape[1:]), EXPERT_AXES)


def sum_half(terms, *earlier):
    return sum_terms(terms, *earlier).astype(BF16)


def sum_along(value, every_axes):
    for axes in every_axes:
        count = lax.axis_size(axes)
        value = tree_sum([value] + [swap_with(value, axes, count, k) for k in range(1, count)])
    return value


def bias_kernel(row_ref, seg_col_ref, seg_row_ref, out_ref):
    offsets = jnp.broadcast_to(row_ref[0], (ROWS, SPAN))
    seg_row = seg_row_ref[...]
    for first in range(0, SEQ, ROWS):
        turned = pltpu.roll(offsets, first, 1, stride=1, stride_axis=0)[:, :SEQ]
        same = seg_col_ref[first : first + ROWS, :] == seg_row
        out_ref[0, first : first + ROWS, :] = jnp.where(same, turned, NEG_FILL)


def offset_onehot():
    columns = jnp.arange(SPAN, dtype=jnp.int32)
    offsets = jnp.where(columns < SEQ, columns, columns - SPAN)
    return (bucket_of(offsets)[:, None] == jnp.arange(BUCKETS, dtype=jnp.int32)[None, :]).astype(F32)


def masked_bias(rel_bias, segments):
    by_offset = jnp.dot(offset_onehot(), rel_bias, precision=PRECISE).T
    return pl.pallas_call(
        bias_kernel,
        grid=(HEADS,),
        in_specs=[
            pl.BlockSpec((1, 1, SPAN), lambda h: (h, 0, 0)),
            pl.BlockSpec((SEQ, 1), lambda h: (0, 0)),
            pl.BlockSpec((1, SEQ), lambda h: (0, 0)),
        ],
        out_specs=pl.BlockSpec((1, SEQ, SEQ), lambda h: (h, 0, 0)),
        out_shape=jax.ShapeDtypeStruct((HEADS, SEQ, SEQ), F32),
        compiler_params=pltpu.CompilerParams(vmem_limit_bytes=VMEM_BYTES),
        cost_estimate=pl.CostEstimate(flops=ATTEND_COST // 3, bytes_accessed=HEADS * SEQ * SEQ * 8, transcendentals=0),
    )(by_offset.reshape(HEADS, 1, SPAN), segments.reshape(SEQ, 1), segments.reshape(1, SEQ))


def dot_nt(a, b):
    return lax.dot_general(a, b, (((1,), (1,)), ((), ())), preferred_element_type=F32)


def dot_tn(a, b):
    return lax.dot_general(a, b, (((0,), (0,)), ((), ())), preferred_element_type=F32)


def stacked_heads(rows):
    lanes = lax.broadcasted_iota(jnp.int32, rows.shape, 1)
    none = jnp.zeros_like(rows)
    return jnp.concatenate([jnp.where(lanes < DH, rows, none), jnp.where(lanes < DH, none, rows)])


def own_columns(stacked):
    rows = stacked.shape[0] // 2
    lanes = lax.broadcasted_iota(jnp.int32, (rows, 2 * DH), 1)
    return jnp.where(lanes < DH, stacked[:rows], stacked[rows:])


def attend_kernel(q_ref, k_ref, v_ref, bias_ref, mixed_ref, prob_ref):
    keys = k_ref[...]
    values = v_ref[...]
    for first in range(0, SEQ, CHUNK):
        rows = slice(first, first + CHUNK)
        query = stacked_heads(q_ref[rows, :] * BF16(DH ** (-0.5)))
        scores = dot_nt(query, keys) + bias_ref[:, rows, :].reshape(2 * CHUNK, SEQ)
        grown = jnp.exp(scores - jnp.max(scores, axis=-1, keepdims=True))
        prob = (grown * (1.0 / jnp.sum(grown, axis=-1, keepdims=True))).astype(BF16)
        prob_ref[:, rows, :] = prob.reshape(2, CHUNK, SEQ)
        mixed = jnp.dot(prob, values, preferred_element_type=F32)
        mixed_ref[rows, :] = own_columns(mixed).astype(BF16)


PAIRS = HEADS // 2


def attend_forward(packed, bias):
    def columns(base):
        return pl.BlockSpec((SEQ, 2 * DH), lambda p: (0, base + p))

    return pl.pallas_call(
        attend_kernel,
        grid=(PAIRS,),
        in_specs=[
            columns(0),
            columns(PAIRS),
            columns(2 * PAIRS),
            pl.BlockSpec((2, SEQ, SEQ), lambda p: (p, 0, 0)),
        ],
        out_specs=[columns(0), pl.BlockSpec((2, SEQ, SEQ), lambda p: (p, 0, 0))],
        out_shape=[
            jax.ShapeDtypeStruct((SEQ, HEADS * DH), BF16),
            jax.ShapeDtypeStruct((HEADS, SEQ, SEQ), BF16),
        ],
        compiler_params=pltpu.CompilerParams(vmem_limit_bytes=VMEM_BYTES),
        cost_estimate=pl.CostEstimate(
            flops=ATTEND_COST, bytes_accessed=SEQ * SEQ, transcendentals=0
        ),
    )(packed, packed, packed, bias)


def attend_back_kernel(q_ref, k_ref, v_ref, grad_ref, prob_ref, out_ref, diag_ref, raw_ref, shift_ref):
    pair = pl.program_id(0)
    keys = k_ref[...]
    values = v_ref[...]
    width = 2 * DH

    def put(base, rows, value):
        spot = pl.multiple_of((base + pair) * width, width)
        out_ref[rows, pl.ds(spot, width)] = value.astype(BF16)

    shift_ref[...] = jnp.zeros_like(shift_ref)
    for first in range(0, SEQ, CHUNK):
        rows = slice(first, first + CHUNK)
        grad_prob = dot_nt(stacked_heads(grad_ref[rows, :]), values)
        prob = prob_ref[:, rows, :].reshape(2 * CHUNK, SEQ).astype(F32)
        weighted = prob * grad_prob
        grad_scores = weighted - prob * jnp.sum(weighted, axis=-1, keepdims=True)
        for head in range(2):
            for block in range(CHUNK // ROWS):
                start = SEQ - first - ROWS * (block + 1)
                origin = head * CHUNK + block * ROWS
                shift_ref[head, :, start : start + SEQ] += grad_scores[origin : origin + ROWS, :]
        raw = (grad_scores * DH ** (-0.5)).astype(BF16)
        raw_ref[:, rows, :] = raw.reshape(2, CHUNK, SEQ)
        put(0, rows, own_columns(jnp.dot(raw, keys, preferred_element_type=F32)))
    query = q_ref[...]
    grads = grad_ref[...]
    everything = slice(0, SEQ)
    grad_key = jnp.concatenate([dot_tn(raw_ref[head], query) for head in range(2)])
    put(PAIRS, everything, own_columns(grad_key))
    grad_value = jnp.concatenate([dot_tn(prob_ref[head], grads) for head in range(2)])
    put(2 * PAIRS, everything, own_columns(grad_value))
    for head in range(2):
        total = shift_ref[head, 0:8, :]
        for group in range(1, ROWS // 8):
            total = total + pltpu.roll(
                shift_ref[head, 8 * group : 8 * group + 8, :], SPAN - 8 * group, 1
            )
        diag_ref[0, head] = total


def attend_backward(packed, grad_mixed, prob):
    def columns(base):
        return pl.BlockSpec((SEQ, 2 * DH), lambda p: (0, base + p))

    width = 3 * HEADS * DH
    return pl.pallas_call(
        attend_back_kernel,
        grid=(PAIRS,),
        in_specs=[
            columns(0),
            columns(PAIRS),
            columns(2 * PAIRS),
            columns(0),
            pl.BlockSpec((2, SEQ, SEQ), lambda p: (p, 0, 0)),
        ],
        out_specs=[
            pl.BlockSpec((SEQ, width), lambda p: (0, 0)),
            pl.BlockSpec((1, 2, 8, SPAN), lambda p: (p, 0, 0, 0)),
        ],
        out_shape=[
            jax.ShapeDtypeStruct((SEQ, width), BF16),
            jax.ShapeDtypeStruct((PAIRS, 2, 8, SPAN), F32),
        ],
        scratch_shapes=[pltpu.VMEM((2, SEQ, SEQ), BF16), pltpu.VMEM((2, ROWS, SPAN), F32)],
        compiler_params=pltpu.CompilerParams(vmem_limit_bytes=VMEM_BYTES),
        cost_estimate=pl.CostEstimate(
            flops=ATTEND_COST, bytes_accessed=SEQ * SEQ, transcendentals=0
        ),
    )(packed, packed, packed, grad_mixed, prob)


def bias_grad(diagonals):
    columns = jnp.arange(SPAN, dtype=jnp.int32)[None, :]
    offsets = columns - jnp.arange(8, dtype=jnp.int32)[:, None] - (SEQ - ROWS)
    offsets = jnp.where(offsets >= SEQ, offsets - SPAN, offsets)
    table = (bucket_of(offsets)[:, :, None] == jnp.arange(BUCKETS, dtype=jnp.int32)).astype(F32)
    return jnp.einsum(
        "hs,sb->bh",
        diagonals.reshape(HEADS, 8 * SPAN),
        table.reshape(8 * SPAN, BUCKETS),
        precision=PRECISE,
    )


def attention_forward(stream, gain_row, qkv_full, out_full, bias):
    normed_low = norm_scale(stream, gain_row.astype(F32)).astype(BF16)
    packed_low = jnp.dot(normed_low, qkv_full, preferred_element_type=F32).astype(BF16)
    mixed_low, prob_low = attend_forward(packed_low, bias)
    stream_after = stream + jnp.dot(mixed_low, out_full, preferred_element_type=F32)
    return (normed_low, packed_low, mixed_low, prob_low, stream_after)


def attention_back_in(grad_stream, out_full, kept_state):
    grad_low = grad_stream.astype(BF16)
    grad_out_w = jnp.einsum("td,te->de", kept_state[2], grad_low, preferred_element_type=F32)
    grad_mixed = jnp.einsum("te,de->td", grad_low, out_full, preferred_element_type=F32)
    return (grad_mixed.astype(BF16), grad_out_w.astype(BF16))


def attention_back_out(packed_grad, grad_stream, stream, gain_row, qkv_full, kept_state):
    grad_normed = jnp.einsum("te,de->td", packed_grad, qkv_full, preferred_element_type=F32)
    grad_input, grad_gain = norm_backward(grad_normed, stream, gain_row)
    return (grad_stream + grad_input, grad_gain)


def qkv_weight_term(packed_grad, kept_state):
    return jnp.einsum("td,te->de", kept_state[0], packed_grad, preferred_element_type=F32).astype(BF16)


def dense_forward(stream, gain_row, weight_in, weight_out):
    normed_low = norm_scale(stream, gain_row.astype(jnp.float32)).astype(jnp.bfloat16)
    hidden_pre = jnp.dot(normed_low, weight_in, preferred_element_type=jnp.float32)
    hidden_low = gelu_tanh(hidden_pre).astype(jnp.bfloat16)
    stream_after = stream + jnp.dot(hidden_low, weight_out, preferred_element_type=jnp.float32)
    return (normed_low, hidden_pre, stream_after)


def dense_back_in(grad_stream, weight_out, kept_state, earlier):
    grad_low = grad_stream.astype(jnp.bfloat16)
    gelu_value, gelu_pull = jax.vjp(gelu_tanh, kept_state[1])
    hidden_low = gelu_value.astype(jnp.bfloat16)
    grad_hidden = (
        jnp.einsum("td,fd->tf", after(grad_low, earlier), weight_out, preferred_element_type=jnp.float32)
        .astype(jnp.bfloat16)
        .astype(jnp.float32)
    )
    grad_pre = gelu_pull(grad_hidden)[0].astype(jnp.bfloat16)
    return (hidden_low, grad_low, grad_pre)


def dense_out_term(hidden_low, grad_low):
    return jnp.einsum(
        "tf,td->fd", hidden_low, grad_low, preferred_element_type=jnp.float32
    ).astype(jnp.bfloat16)


def dense_back_out(grad_stream, stream, gain_row, weight_in, grad_pre, kept_state):
    grad_w_in = jnp.einsum("td,tf->df", kept_state[0], grad_pre, preferred_element_type=jnp.float32)
    grad_normed = jnp.einsum("tf,df->td", grad_pre, weight_in, preferred_element_type=jnp.float32)
    grad_input, grad_gain = norm_backward(grad_normed, stream, gain_row)
    return (grad_stream + grad_input, grad_gain, grad_w_in.astype(jnp.bfloat16))


def dispatch_table(expert_ids, slot_ids, expert_count, capacity):
    target = jnp.where(slot_ids < capacity, expert_ids * capacity + slot_ids, -1)
    return (
        target[:, None] == jnp.arange(expert_count * capacity, dtype=jnp.int32)[None, :]
    ).astype(jnp.bfloat16)


def to_experts(slot_table, rows, experts_here):
    outgoing = jnp.einsum("ts,td->sd", slot_table, rows, preferred_element_type=F32).astype(BF16)
    expert_count = lax.axis_size(EXPERT_AXES) * experts_here
    capacity = rows.shape[0] // expert_count
    outgoing = outgoing.reshape(expert_count // experts_here, experts_here, capacity, -1)
    return lax.all_to_all(outgoing, EXPERT_AXES, split_axis=0, concat_axis=0, tiled=True)


def sparse_layer(
    stream, grad_stream, gain_row, router_full, in_full, out_experts, expert_ids, slot_ids
):
    normed_low = norm_scale(stream, gain_row.astype(F32)).astype(BF16)
    logits = jnp.dot(normed_low, router_full, preferred_element_type=F32)
    expert_count = router_full.shape[1]
    chosen = (expert_ids[:, None] == jnp.arange(expert_count, dtype=jnp.int32)[None, :]).astype(F32)
    gate_values = gate_of(logits, chosen)
    slot_table = dispatch_table(
        expert_ids, slot_ids, expert_count, stream.shape[0] // expert_count
    )
    grad_combined = (gate_values[:, None] * grad_stream).astype(BF16)
    received = to_experts(slot_table, normed_low, in_full.shape[0])
    grad_combined = after(grad_combined, received)
    grad_produced = to_experts(slot_table, grad_combined, in_full.shape[0])

    hidden_pre = jnp.einsum("secd,edf->secf", received, in_full, preferred_element_type=F32)
    gelu_value, gelu_pull = jax.vjp(gelu_tanh, hidden_pre)
    hidden_low = gelu_value.astype(BF16)
    produced = jnp.einsum(
        "secf,efd->secd", hidden_low, out_experts, preferred_element_type=F32
    ).astype(BF16)
    produced, grad_produced = together(produced, grad_produced)
    returned = lax.all_to_all(produced, EXPERT_AXES, split_axis=0, concat_axis=0, tiled=True)

    grad_hidden = (
        jnp.einsum("secd,efd->secf", grad_produced, out_experts, preferred_element_type=F32)
        .astype(BF16)
        .astype(F32)
    )
    grad_pre = gelu_pull(grad_hidden)[0].astype(BF16)
    grad_received = jnp.einsum(
        "secf,edf->secd", grad_pre, in_full, preferred_element_type=F32
    ).astype(BF16)
    returned, grad_received = together(returned, grad_received)
    grad_sent = lax.all_to_all(grad_received, EXPERT_AXES, split_axis=0, concat_axis=0, tiled=True)
    grad_w_out = jnp.einsum("secf,secd->efd", hidden_low, grad_produced, preferred_element_type=F32)

    combined = jnp.dot(
        slot_table, returned.reshape(slot_table.shape[1], -1), preferred_element_type=F32
    )
    stream_after = stream + gate_values[:, None] * combined
    grad_gates = jnp.sum(grad_stream * combined, axis=-1)
    gate_again, gate_pull = jax.vjp(gate_of, logits, chosen)
    grad_logits = gate_pull(grad_gates)[0].astype(BF16)
    grad_router = jnp.einsum("td,te->de", normed_low, grad_logits, preferred_element_type=F32)

    grad_sent, grad_w_out = together(grad_sent, grad_w_out.astype(BF16))
    grad_normed = jnp.dot(
        slot_table, grad_sent.reshape(slot_table.shape[1], -1), preferred_element_type=F32
    )
    grad_normed = grad_normed + jnp.einsum(
        "te,de->td", grad_logits, router_full, preferred_element_type=F32
    )
    grad_input, grad_gain = norm_backward(grad_normed, stream, gain_row)
    return (
        stream_after,
        grad_stream + grad_input,
        grad_gain,
        grad_router,
        (received, grad_pre),
        grad_w_out,
    )


def expert_weight_term(received, grad_pre):
    return jnp.einsum("secd,secf->edf", received, grad_pre, preferred_element_type=F32).astype(BF16)


def on_device(
    tokens_in,
    segment_ids,
    expert_index,
    expert_slot,
    attn_gain,
    qkv_weight,
    out_weight,
    rel_bias,
    ffn_gain,
    ffn_in,
    ffn_out,
    router,
    expert_in,
    expert_out,
    cotangent,
):
    width = tokens_in.shape[1]
    packed_width = qkv_weight.shape[2]
    expert_count = router.shape[1]
    small = jnp.concatenate([attn_gain.T, ffn_gain.T, router], axis=1)
    small_width = -(-small.shape[1] // 128) * 128
    small = jnp.pad(small, ((0, 0), (0, small_width - small.shape[1])))
    joined = packed_width + width
    hidden_width = ffn_in.shape[1]
    rows = ffn_in.shape[0]
    stack = ffn_out.shape[0] // rows
    first_shard = jnp.concatenate([qkv_weight[:, 0], out_weight[:, 0], small], axis=1)
    last_shard = jnp.concatenate([qkv_weight[:, 1], out_weight[:, 1]], axis=1)
    dense_shard = jnp.concatenate(
        [ffn_in] + [ffn_out[i * rows : (i + 1) * rows] for i in range(stack)], axis=1
    )
    first_line = gather_z(send_z(first_shard))
    first_across = send_across(first_line)
    rest_shard = jnp.concatenate([dense_shard, last_shard], axis=1)
    dense_width = dense_shard.shape[1]
    dense_line, last_line = gather_z(
        send_z(after(rest_shard, first_line), first_across[1]),
        (((0, dense_width),), ((dense_width, dense_width + last_shard.shape[1]),)),
    )
    bias = masked_bias(rel_bias, after(segment_ids, first_line))
    first_half = gather_across(first_across)
    first_half, dense_line, last_line, bias, expert_in, expert_out = together(
        first_half, dense_line, last_line, bias, expert_in, expert_out
    )
    in_full = lax.all_gather(expert_in, DATA_AXES, axis=1, tiled=True)
    out_experts = lax.all_gather(expert_out, DATA_AXES, axis=1, tiled=True)
    qkv_zero, out_zero, small_full = gather_core(
        first_half,
        (((0, packed_width),), ((packed_width, joined),), ((joined, joined + small_width),)),
    )
    gains = small_full[:, :4].T
    router_full = small_full[:, 4 : 4 + expert_count]

    stream_zero = tokens_in.astype(F32)
    attn_zero = attention_forward(stream_zero, gains[0], qkv_zero, out_zero, bias)
    dense_half = gather_across(send_around(dense_line, attn_zero[2]), attn_zero[2])
    ffn_in_full, ffn_out_full = gather_core(
        dense_half,
        (
            ((0, hidden_width),),
            tuple((hidden_width + i * width, hidden_width + (i + 1) * width) for i in range(stack)),
        ),
        attn_zero[4],
    )
    dense_zero = dense_forward(attn_zero[4], gains[2], ffn_in_full, ffn_out_full)
    last_half = gather_across(send_across(after(last_line, dense_half)), dense_zero[1])
    qkv_one, out_one = gather_core(
        last_half, (((0, packed_width),), ((packed_width, joined),)), dense_zero[2]
    )
    attn_one = attention_forward(dense_zero[2], gains[1], qkv_one, out_one, bias)
    (
        stream_two,
        grad_middle,
        ffn_gain_one,
        router_term,
        expert_in_rows,
        expert_out_term,
    ) = sparse_layer(
        attn_one[4],
        cotangent.astype(F32),
        gains[3],
        router_full,
        in_full,
        out_experts,
        expert_index,
        expert_slot,
    )
    expert_in_rows = together(*expert_in_rows, expert_out_term)
    expert_in_term = expert_weight_term(*expert_in_rows[:2])
    grad_middle, expert_in_term = together(grad_middle, expert_in_term)
    expert_out_sum = lax.psum_scatter(
        expert_out_term, DATA_AXES, scatter_dimension=1, tiled=True
    )
    expert_in_sum = lax.psum_scatter(
        expert_in_term, DATA_AXES, scatter_dimension=1, tiled=True
    )

    grad_mixed_one, out_one_term = attention_back_in(grad_middle, out_one, attn_one)
    packed_grad_one, pairs_one = attend_backward(attn_one[1], grad_mixed_one, attn_one[3])
    qkv_one_term = qkv_weight_term(packed_grad_one, attn_one)
    grad_one, attn_gain_one = attention_back_out(
        packed_grad_one, grad_middle, dense_zero[2], gains[1], qkv_one, attn_one
    )
    last_half = scatter_core([qkv_one_term, out_one_term])
    hidden_low, grad_low, grad_pre = dense_back_in(grad_one, ffn_out_full, dense_zero, last_half)
    last_terms = send_half(last_half)
    ffn_out_term = dense_out_term(hidden_low, grad_low)
    back_half = scatter_core([ffn_out_term])
    back_half, grad_pre, last_terms = together(back_half, grad_pre, last_terms)
    back_terms = send_half(back_half)
    grad_half, ffn_gain_zero, ffn_in_term = dense_back_out(
        grad_one, attn_zero[4], gains[2], ffn_in_full, grad_pre, dense_zero
    )
    grad_mixed_zero, out_zero_term = attention_back_in(grad_half, out_zero, attn_zero)
    into_half = scatter_core([ffn_in_term])
    into_half, grad_mixed_zero = together(into_half, grad_mixed_zero)
    packed_grad_zero, pairs_zero = attend_backward(attn_zero[1], grad_mixed_zero, attn_zero[3])
    qkv_zero_term = qkv_weight_term(packed_grad_zero, attn_zero)
    first_half = scatter_core([qkv_zero_term, out_zero_term])
    into_half, back_terms, packed_grad_zero, pairs_zero = together(
        into_half, back_terms, packed_grad_zero, pairs_zero
    )
    into_terms = send_half(into_half)
    ffn_out_sum = sum_z(sum_half(back_terms))
    grad_zero, attn_gain_zero = attention_back_out(
        packed_grad_zero, grad_half, stream_zero, gains[0], qkv_zero, attn_zero
    )
    first_half, into_terms, ffn_out_sum, grad_zero, pairs_zero, last_terms = together(
        first_half, into_terms, ffn_out_sum, grad_zero, pairs_zero, last_terms
    )
    first_terms = send_half(first_half)
    tiny = jnp.concatenate(
        [
            attn_gain_zero,
            attn_gain_one,
            ffn_gain_zero,
            ffn_gain_one,
            router_term.reshape(-1),
            bias_grad(pairs_zero + pairs_one).reshape(-1),
        ]
    )
    tiny_sum = sum_along(tiny.reshape(-1, 128), ("core",))
    expert_in_sum, expert_out_sum, into_terms, last_terms = together(
        expert_in_sum, expert_out_sum, into_terms, last_terms
    )
    later_line = jnp.concatenate([sum_half(into_terms), sum_half(last_terms)], axis=-1)
    later_sum = sum_z(later_line)
    tiny_sum, first_terms, later_sum = together(tiny_sum, first_terms, later_sum)
    ffn_in_sum = later_sum[:, :hidden_width]
    one_sum = later_sum[:, hidden_width:]
    tiny_sum = sum_along(tiny_sum, (EXPERT_AXES, "z")).reshape(-1)
    zero_sum = sum_z(sum_half(first_terms))
    qkv_sum = jnp.stack([zero_sum[:, :packed_width], one_sum[:, :packed_width]], axis=1)
    out_sum = jnp.stack([zero_sum[:, packed_width:], one_sum[:, packed_width:]], axis=1)

    gain_sums = tiny_sum[: 4 * width].reshape(4, width)
    router_sums = tiny_sum[4 * width : (4 + expert_count) * width].reshape(width, expert_count)
    bias_sum = tiny_sum[(4 + expert_count) * width :].reshape(BUCKETS, HEADS)
    first_row = lax.axis_index(ALL_AXES) * rows
    gain_shard = lax.dynamic_slice_in_dim(gain_sums, first_row, rows, 1)
    router_shard = lax.dynamic_slice_in_dim(router_sums, first_row, rows, 0)
    return (
        stream_two.astype(BF16),
        grad_zero,
        gain_shard[:2],
        qkv_sum,
        out_sum,
        bias_sum,
        gain_shard[2:],
        ffn_in_sum,
        ffn_out_sum,
        router_shard,
        expert_in_sum.astype(F32),
        expert_out_sum.astype(F32),
    )


def solution(mesh):
    experts, data = mesh.shape["expert"], mesh.shape["dp"]
    side = 1 << ((experts.bit_length() - 1) // 2)
    fine = Mesh(mesh.devices.reshape(experts // side, side, data // 2, 2), ALL_AXES)
    placed = (
        P(ALL_AXES, None),
        P(ALL_AXES, None),
        P(ALL_AXES),
        P(ALL_AXES),
        P(None, ALL_AXES),
        P(ALL_AXES, None, None),
        P(ALL_AXES, None, None),
        P(),
        P(None, ALL_AXES),
        P(ALL_AXES, None),
        P(ALL_AXES, None),
        P(ALL_AXES, None),
        P(EXPERT_AXES, DATA_AXES, None),
        P(EXPERT_AXES, DATA_AXES, None),
        P(ALL_AXES, None),
    )
    return jax.shard_map(
        on_device,
        mesh=fine,
        in_specs=placed,
        out_specs=(
            P(ALL_AXES, None),
            P(ALL_AXES, None),
            P(None, ALL_AXES),
            P(ALL_AXES, None, None),
            P(ALL_AXES, None, None),
            P(),
            P(None, ALL_AXES),
            P(ALL_AXES, None),
            P(ALL_AXES, None),
            P(ALL_AXES, None),
            P(EXPERT_AXES, DATA_AXES, None),
            P(EXPERT_AXES, DATA_AXES, None),
        ),
        check_vma=False,
    )
```

```python
import functools
import math

import jax
import jax.numpy as jnp
from jax import lax
from jax.experimental import pallas as pl
from jax.experimental.pallas import tpu as pltpu
from jax.sharding import Mesh, PartitionSpec as P

HEADS = 12
DH = 64
BUCKETS = 32
SEQ = 512


EPSILON = 1e-06
NEG_FILL = -1e30
PRECISE = lax.Precision.HIGHEST


def bucket_of(offset):
    distance = jnp.abs(offset)
    far_bucket = jnp.full_like(distance, 8)
    for level_id in range(1, 8):
        far_bucket = far_bucket + (distance * distance >= 64 * 2**level_id).astype(jnp.int32)
    near_bucket = jnp.where(distance < 8, distance, far_bucket)
    return near_bucket + 16 * (offset > 0).astype(jnp.int32)


def norm_scale(stream, gain_row):
    inverse = lax.rsqrt(jnp.mean(stream * stream, axis=-1, keepdims=True) + EPSILON)
    return stream * inverse * gain_row


def norm_backward(grad_normed, stream, gain_row):
    normed_again, norm_pull = jax.vjp(norm_scale, stream, gain_row.astype(jnp.float32))
    grad_input, grad_gain = norm_pull(grad_normed)
    return (grad_input, grad_gain)


def gelu_tanh(value):
    return jax.nn.gelu(value, approximate=True)


def gate_of(logits, chosen):
    return jnp.sum(jax.nn.softmax(logits, axis=-1) * chosen, axis=-1)


EXPERT_AXES = ("ey", "ex")
DATA_AXES = ("z", "core")
ALL_AXES = ("ey", "ex", "z", "core")
SPAN = 2 * SEQ
ROWS = 128
CHUNK = 256
VMEM_BYTES = 24 * 1024 * 1024
BF16 = jnp.bfloat16
F32 = jnp.float32
ATTEND_COST = HEADS * SEQ * SEQ


def swap_with(value, axes, count, flip):
    return lax.ppermute(value, axes, [(i, i ^ flip) for i in range(count)])


def place_kernel(count, pieces, axis, cuts, me_ref, *refs):
    sources = refs[: len(pieces)]
    targets = refs[len(pieces) : len(pieces) + len(cuts)]
    held, in_sems, out_sems = refs[len(pieces) + len(cuts) :]
    arriving = [[] for flip in range(count)]
    for source_id, (flip, first, rows) in enumerate(pieces):
        spot = held.at[flip]
        if rows:
            spot = spot.at[first : first + rows]
        copy = pltpu.make_async_copy(sources[source_id], spot, in_sems.at[source_id])
        copy.start()
        arriving[flip].append(copy)
    leaving = []
    for flip in range(count):
        slot = me_ref[0] ^ flip
        for copy in arriving[flip]:
            copy.wait()
        for cut_id, group in enumerate(cuts):
            target = targets[cut_id]
            target = target.at[slot] if axis == 0 else target.at[:, slot]
            for part_id, (first, last) in enumerate(group):
                origin = held.at[flip]
                if axis == 1:
                    origin = origin.at[:, :, first:last]
                elif len(cuts) > 1:
                    origin = origin.at[:, first:last]
                spot = target if len(group) == 1 else target.at[:, part_id]
                copy = pltpu.make_async_copy(origin, spot, out_sems.at[flip, cut_id, part_id])
                copy.start()
                leaving.append(copy)
    for copy in leaving:
        copy.wait()


def room_for(elements, rows):
    return elements // rows * (-(-rows // 16) * 16) * 2 + (1 << 20)


def place(parts, me, axis=0, cuts=None):
    sources, pieces = [], []
    for flip, part in enumerate(parts):
        first = 0
        for piece in part if isinstance(part, list) else [part]:
            pieces.append((flip, first, piece.shape[0] if isinstance(part, list) else 0))
            sources.append(piece)
            first += piece.shape[0]
    shape = parts[0].shape
    groups = cuts or (((0, shape[-1]),),)
    outs = []
    for group in groups:
        own = shape[:-1] + (group[0][1] - group[0][0],)
        lead = own[:axis] + (len(parts),) + ((len(group),) if len(group) > 1 else ())
        outs.append(jax.ShapeDtypeStruct(lead + own[axis:], parts[0].dtype))
    moved = sum(math.prod(o.shape) for o in outs) * 4
    most = max(len(group) for group in groups)
    placed = pl.pallas_call(
        functools.partial(place_kernel, len(parts), tuple(pieces), axis, groups),
        out_shape=outs,
        in_specs=[pl.BlockSpec(memory_space=pltpu.SMEM)]
        + [pl.BlockSpec(memory_space=pl.ANY)] * len(sources),
        out_specs=[pl.BlockSpec(memory_space=pl.ANY)] * len(outs),
        scratch_shapes=[
            pltpu.VMEM((len(parts),) + shape, parts[0].dtype),
            pltpu.SemaphoreType.DMA((len(sources),)),
            pltpu.SemaphoreType.DMA((len(parts), len(groups), most)),
        ],
        compiler_params=pltpu.CompilerParams(
            vmem_limit_bytes=room_for(math.prod(shape) * len(parts), shape[-2])
        ),
        cost_estimate=pl.CostEstimate(flops=0, bytes_accessed=2 * moved, transcendentals=0),
    )(me.astype(jnp.int32).reshape(1), *sources)
    return placed if cuts else placed[0]


def together(*values):
    return lax.optimization_barrier(values)


def after(value, *earlier):
    return lax.optimization_barrier((value,) + earlier)[0]


def send_z(shard, *earlier):
    depth = lax.axis_size("z")
    along = [shard] + [swap_with(shard, "z", depth, k) for k in range(1, depth - 1)]
    last = after(shard, *earlier) if earlier else shard
    return along + [swap_with(last, "z", depth, depth - 1)]


def gather_z(along, cuts=None):
    return place(along, lax.axis_index("z"), cuts=cuts)


def send_across(line):
    experts = lax.axis_size(EXPERT_AXES)
    return [line] + [swap_with(line, EXPERT_AXES, experts, k) for k in range(1, experts)]


def send_around(line, *earlier):
    if lax.axis_size("ey") != 2 or lax.axis_size("ex") != 2:
        return send_across(line)
    near_x = swap_with(line, "ex", 2, 1)
    near_y = swap_with(line, "ey", 2, 1)
    middle = line.shape[0] // 2
    from_x, from_y = together(near_x, near_y, *earlier)[:2]
    far = [
        swap_with(from_x[:middle], "ey", 2, 1),
        swap_with(from_y[middle:], "ex", 2, 1),
    ]
    return [line, near_x, near_y, far]


def gather_across(across, *earlier):
    if earlier:
        across = [across[0], after(across[1], *earlier)] + across[2:]
    half = place(across, lax.axis_index(EXPERT_AXES))
    return half.reshape((-1,) + half.shape[2:])


def gather_core(half, cuts, *earlier):
    other = swap_with(half, "core", 2, 1)
    if earlier:
        other = after(other, *earlier)
    whole = place([half, other], lax.axis_index("core"), axis=1, cuts=cuts)
    return [part.reshape(-1, part.shape[-1]) for part in whole]


def tree_sum(terms):
    while len(terms) > 1:
        terms = [terms[i] + terms[i + 1] for i in range(0, len(terms), 2)]
    return terms[0]


def exchange(whole, axes):
    return lax.all_to_all(whole, axes, split_axis=0, concat_axis=0, tiled=True)


def sum_z(line):
    depth = lax.axis_size("z")
    me = lax.axis_index("z")
    terms = [lax.dynamic_index_in_dim(line, me, 0, keepdims=False)]
    for flip in range(1, depth):
        block = lax.dynamic_index_in_dim(line, me ^ flip, 0, keepdims=False)
        terms.append(swap_with(block, "z", depth, flip))
    return tree_sum([t.astype(F32) for t in terms])


def sum_terms(terms, *earlier):
    if earlier:
        terms = after(terms, *earlier)
    return jnp.sum(terms.astype(F32), axis=0)


def split_kernel(widths, me_ref, *refs):
    count = len(widths)
    sources = refs[:count]
    targets = refs[count : count + 2]
    held, in_sems, out_sems = refs[count + 2 :]
    arriving = []
    for flip in range(2):
        slot = me_ref[0] ^ flip
        first = 0
        for part_id, width in enumerate(widths):
            spot = held.at[flip]
            if count > 1:
                spot = spot.at[:, :, first : first + width]
            copy = pltpu.make_async_copy(sources[part_id].at[:, slot], spot, in_sems.at[flip, part_id])
            copy.start()
            arriving.append(copy)
            first += width
    leaving = []
    for flip in range(2):
        for copy in arriving[flip * count : (flip + 1) * count]:
            copy.wait()
        copy = pltpu.make_async_copy(held.at[flip], targets[flip], out_sems.at[flip])
        copy.start()
        leaving.append(copy)
    for copy in leaving:
        copy.wait()


def scatter_core(grads, *earlier):
    groups = lax.axis_size(EXPERT_AXES) * lax.axis_size("z")
    pieces = [g.reshape(groups, 2, g.shape[0] // (2 * groups), g.shape[1]) for g in grads]
    widths = tuple(g.shape[1] for g in grads)
    out = jax.ShapeDtypeStruct((groups, pieces[0].shape[2], sum(widths)), BF16)
    kept, sent = pl.pallas_call(
        functools.partial(split_kernel, widths),
        out_shape=[out, out],
        in_specs=[pl.BlockSpec(memory_space=pltpu.SMEM)]
        + [pl.BlockSpec(memory_space=pl.ANY)] * len(pieces),
        out_specs=[pl.BlockSpec(memory_space=pl.ANY)] * 2,
        scratch_shapes=[
            pltpu.VMEM((2,) + out.shape, BF16),
            pltpu.SemaphoreType.DMA((2, len(pieces))),
            pltpu.SemaphoreType.DMA((2,)),
        ],
        compiler_params=pltpu.CompilerParams(
            vmem_limit_bytes=room_for(2 * math.prod(out.shape), out.shape[-2])
        ),
        cost_estimate=pl.CostEstimate(
            flops=0, bytes_accessed=math.prod(out.shape) // 4, transcendentals=0
        ),
    )(lax.axis_index("core").astype(jnp.int32).reshape(1), *pieces)
    other = swap_with(sent, "core", 2, 1)
    if earlier:
        other = after(other, *earlier)
    return (kept.astype(F32) + other.astype(F32)).astype(BF16)


def send_half(half):
    experts = lax.axis_size(EXPERT_AXES)
    return exchange(half.reshape((experts, -1) + half.shape[1:]), EXPERT_AXES)


def sum_half(terms, *earlier):
    return sum_terms(terms, *earlier).astype(BF16)


def sum_along(value, every_axes):
    for axes in every_axes:
        count = lax.axis_size(axes)
        value = tree_sum([value] + [swap_with(value, axes, count, k) for k in range(1, count)])
    return value


def bias_kernel(row_ref, seg_col_ref, seg_row_ref, out_ref):
    offsets = jnp.broadcast_to(row_ref[0], (ROWS, SPAN))
    seg_row = seg_row_ref[...]
    for first in range(0, SEQ, ROWS):
        turned = pltpu.roll(offsets, first, 1, stride=1, stride_axis=0)[:, :SEQ]
        same = seg_col_ref[first : first + ROWS, :] == seg_row
        out_ref[0, first : first + ROWS, :] = jnp.where(same, turned, NEG_FILL)


def offset_onehot():
    columns = jnp.arange(SPAN, dtype=jnp.int32)
    offsets = jnp.where(columns < SEQ, columns, columns - SPAN)
    return (bucket_of(offsets)[:, None] == jnp.arange(BUCKETS, dtype=jnp.int32)[None, :]).astype(F32)


def masked_bias(rel_bias, segments):
    by_offset = jnp.dot(offset_onehot(), rel_bias, precision=PRECISE).T
    return pl.pallas_call(
        bias_kernel,
        grid=(HEADS,),
        in_specs=[
            pl.BlockSpec((1, 1, SPAN), lambda h: (h, 0, 0)),
            pl.BlockSpec((SEQ, 1), lambda h: (0, 0)),
            pl.BlockSpec((1, SEQ), lambda h: (0, 0)),
        ],
        out_specs=pl.BlockSpec((1, SEQ, SEQ), lambda h: (h, 0, 0)),
        out_shape=jax.ShapeDtypeStruct((HEADS, SEQ, SEQ), F32),
        compiler_params=pltpu.CompilerParams(vmem_limit_bytes=VMEM_BYTES),
        cost_estimate=pl.CostEstimate(flops=ATTEND_COST // 3, bytes_accessed=HEADS * SEQ * SEQ * 8, transcendentals=0),
    )(by_offset.reshape(HEADS, 1, SPAN), segments.reshape(SEQ, 1), segments.reshape(1, SEQ))


def dot_nt(a, b):
    return lax.dot_general(a, b, (((1,), (1,)), ((), ())), preferred_element_type=F32)


def dot_tn(a, b):
    return lax.dot_general(a, b, (((0,), (0,)), ((), ())), preferred_element_type=F32)


def weight_term_kernel(rows_ref, grad_ref, out_ref, turned_ref):
    @pl.when(pl.program_id(0) == 0)
    def _():
        turned_ref[...] = rows_ref[...].T

    out_ref[...] = jnp.dot(turned_ref[...], grad_ref[...], preferred_element_type=F32).astype(BF16)


def weight_term(rows, grads):
    tokens, depth = rows.shape
    width = grads.shape[1]
    block = 512 if width % 512 == 0 else width
    return pl.pallas_call(
        weight_term_kernel,
        grid=(width // block,),
        in_specs=[
            pl.BlockSpec((tokens, depth), lambda i: (0, 0)),
            pl.BlockSpec((tokens, block), lambda i: (0, i)),
        ],
        out_specs=pl.BlockSpec((depth, block), lambda i: (0, i)),
        out_shape=jax.ShapeDtypeStruct((depth, width), BF16),
        scratch_shapes=[pltpu.VMEM((depth, tokens), BF16)],
        compiler_params=pltpu.CompilerParams(vmem_limit_bytes=VMEM_BYTES),
        cost_estimate=pl.CostEstimate(
            flops=ATTEND_COST, bytes_accessed=SEQ * SEQ, transcendentals=0
        ),
    )(rows, grads)


def stacked_heads(rows):
    lanes = lax.broadcasted_iota(jnp.int32, rows.shape, 1)
    none = jnp.zeros_like(rows)
    return jnp.concatenate([jnp.where(lanes < DH, rows, none), jnp.where(lanes < DH, none, rows)])


def own_columns(stacked):
    rows = stacked.shape[0] // 2
    lanes = lax.broadcasted_iota(jnp.int32, (rows, 2 * DH), 1)
    return jnp.where(lanes < DH, stacked[:rows], stacked[rows:])


def attend_kernel(q_ref, k_ref, v_ref, bias_ref, mixed_ref, prob_ref):
    keys = k_ref[...]
    values = v_ref[...]
    for first in range(0, SEQ, CHUNK):
        rows = slice(first, first + CHUNK)
        query = stacked_heads(q_ref[rows, :] * BF16(DH ** (-0.5)))
        scores = dot_nt(query, keys) + bias_ref[:, rows, :].reshape(2 * CHUNK, SEQ)
        grown = jnp.exp(scores - jnp.max(scores, axis=-1, keepdims=True))
        prob = (grown * (1.0 / jnp.sum(grown, axis=-1, keepdims=True))).astype(BF16)
        prob_ref[:, rows, :] = prob.reshape(2, CHUNK, SEQ)
        mixed = jnp.dot(prob, values, preferred_element_type=F32)
        mixed_ref[rows, :] = own_columns(mixed).astype(BF16)


PAIRS = HEADS // 2


def attend_forward(packed, bias):
    def columns(base):
        return pl.BlockSpec((SEQ, 2 * DH), lambda p: (0, base + p))

    return pl.pallas_call(
        attend_kernel,
        grid=(PAIRS,),
        in_specs=[
            columns(0),
            columns(PAIRS),
            columns(2 * PAIRS),
            pl.BlockSpec((2, SEQ, SEQ), lambda p: (p, 0, 0)),
        ],
        out_specs=[columns(0), pl.BlockSpec((2, SEQ, SEQ), lambda p: (p, 0, 0))],
        out_shape=[
            jax.ShapeDtypeStruct((SEQ, HEADS * DH), BF16),
            jax.ShapeDtypeStruct((HEADS, SEQ, SEQ), BF16),
        ],
        compiler_params=pltpu.CompilerParams(vmem_limit_bytes=VMEM_BYTES),
        cost_estimate=pl.CostEstimate(
            flops=ATTEND_COST, bytes_accessed=SEQ * SEQ, transcendentals=0
        ),
    )(packed, packed, packed, bias)


def attend_back_kernel(q_ref, k_ref, v_ref, grad_ref, prob_ref, out_ref, diag_ref, raw_ref, shift_ref):
    pair = pl.program_id(0)
    keys = k_ref[...]
    values = v_ref[...]
    width = 2 * DH

    def put(base, rows, value):
        spot = pl.multiple_of((base + pair) * width, width)
        out_ref[rows, pl.ds(spot, width)] = value.astype(BF16)

    shift_ref[...] = jnp.zeros_like(shift_ref)
    for first in range(0, SEQ, CHUNK):
        rows = slice(first, first + CHUNK)
        grad_prob = dot_nt(stacked_heads(grad_ref[rows, :]), values)
        prob = prob_ref[:, rows, :].reshape(2 * CHUNK, SEQ).astype(F32)
        weighted = prob * grad_prob
        grad_scores = weighted - prob * jnp.sum(weighted, axis=-1, keepdims=True)
        for head in range(2):
            for block in range(CHUNK // ROWS):
                start = SEQ - first - ROWS * (block + 1)
                origin = head * CHUNK + block * ROWS
                shift_ref[head, :, start : start + SEQ] += grad_scores[origin : origin + ROWS, :]
        raw = (grad_scores * DH ** (-0.5)).astype(BF16)
        raw_ref[:, rows, :] = raw.reshape(2, CHUNK, SEQ)
        put(0, rows, own_columns(jnp.dot(raw, keys, preferred_element_type=F32)))
    query = q_ref[...]
    grads = grad_ref[...]
    everything = slice(0, SEQ)
    grad_key = jnp.concatenate([dot_tn(raw_ref[head], query) for head in range(2)])
    put(PAIRS, everything, own_columns(grad_key))
    grad_value = jnp.concatenate([dot_tn(prob_ref[head], grads) for head in range(2)])
    put(2 * PAIRS, everything, own_columns(grad_value))
    for head in range(2):
        total = shift_ref[head, 0:8, :]
        for group in range(1, ROWS // 8):
            total = total + pltpu.roll(
                shift_ref[head, 8 * group : 8 * group + 8, :], SPAN - 8 * group, 1
            )
        diag_ref[0, head] = total


def attend_backward(packed, grad_mixed, prob):
    def columns(base):
        return pl.BlockSpec((SEQ, 2 * DH), lambda p: (0, base + p))

    width = 3 * HEADS * DH
    return pl.pallas_call(
        attend_back_kernel,
        grid=(PAIRS,),
        in_specs=[
            columns(0),
            columns(PAIRS),
            columns(2 * PAIRS),
            columns(0),
            pl.BlockSpec((2, SEQ, SEQ), lambda p: (p, 0, 0)),
        ],
        out_specs=[
            pl.BlockSpec((SEQ, width), lambda p: (0, 0)),
            pl.BlockSpec((1, 2, 8, SPAN), lambda p: (p, 0, 0, 0)),
        ],
        out_shape=[
            jax.ShapeDtypeStruct((SEQ, width), BF16),
            jax.ShapeDtypeStruct((PAIRS, 2, 8, SPAN), F32),
        ],
        scratch_shapes=[pltpu.VMEM((2, SEQ, SEQ), BF16), pltpu.VMEM((2, ROWS, SPAN), F32)],
        compiler_params=pltpu.CompilerParams(vmem_limit_bytes=VMEM_BYTES),
        cost_estimate=pl.CostEstimate(
            flops=ATTEND_COST, bytes_accessed=SEQ * SEQ, transcendentals=0
        ),
    )(packed, packed, packed, grad_mixed, prob)


def bias_grad(diagonals):
    columns = jnp.arange(SPAN, dtype=jnp.int32)[None, :]
    offsets = columns - jnp.arange(8, dtype=jnp.int32)[:, None] - (SEQ - ROWS)
    offsets = jnp.where(offsets >= SEQ, offsets - SPAN, offsets)
    table = (bucket_of(offsets)[:, :, None] == jnp.arange(BUCKETS, dtype=jnp.int32)).astype(F32)
    return jnp.einsum(
        "hs,sb->bh",
        diagonals.reshape(HEADS, 8 * SPAN),
        table.reshape(8 * SPAN, BUCKETS),
        precision=PRECISE,
    )


def attention_forward(stream, gain_row, qkv_full, out_full, bias):
    normed_low = norm_scale(stream, gain_row.astype(F32)).astype(BF16)
    packed_low = jnp.dot(normed_low, qkv_full, preferred_element_type=F32).astype(BF16)
    mixed_low, prob_low = attend_forward(packed_low, bias)
    stream_after = stream + jnp.dot(mixed_low, out_full, preferred_element_type=F32)
    return (normed_low, packed_low, mixed_low, prob_low, stream_after)


def attention_back_in(grad_stream, out_full, kept_state):
    grad_low = grad_stream.astype(BF16)
    grad_out_w = jnp.einsum("td,te->de", kept_state[2], grad_low, preferred_element_type=F32)
    grad_mixed = jnp.einsum("te,de->td", grad_low, out_full, preferred_element_type=F32)
    return (grad_mixed.astype(BF16), grad_out_w.astype(BF16))


def attention_back_out(packed_grad, grad_stream, stream, gain_row, qkv_full, kept_state):
    grad_normed = jnp.einsum("te,de->td", packed_grad, qkv_full, preferred_element_type=F32)
    grad_input, grad_gain = norm_backward(grad_normed, stream, gain_row)
    return (grad_stream + grad_input, grad_gain)


def qkv_weight_term(packed_grad, kept_state):
    return jnp.einsum("td,te->de", kept_state[0], packed_grad, preferred_element_type=F32).astype(BF16)


def dense_forward(stream, gain_row, weight_in, weight_out):
    normed_low = norm_scale(stream, gain_row.astype(jnp.float32)).astype(jnp.bfloat16)
    hidden_pre = jnp.dot(normed_low, weight_in, preferred_element_type=jnp.float32)
    hidden_low = gelu_tanh(hidden_pre).astype(jnp.bfloat16)
    stream_after = stream + jnp.dot(hidden_low, weight_out, preferred_element_type=jnp.float32)
    return (normed_low, hidden_pre, stream_after)


def dense_back_in(grad_stream, weight_out, kept_state, earlier):
    grad_low = grad_stream.astype(jnp.bfloat16)
    gelu_value, gelu_pull = jax.vjp(gelu_tanh, kept_state[1])
    hidden_low = gelu_value.astype(jnp.bfloat16)
    grad_hidden = (
        jnp.einsum("td,fd->tf", after(grad_low, earlier), weight_out, preferred_element_type=jnp.float32)
        .astype(jnp.bfloat16)
        .astype(jnp.float32)
    )
    grad_pre = gelu_pull(grad_hidden)[0].astype(jnp.bfloat16)
    return (hidden_low, grad_low, grad_pre)


def dense_out_term(hidden_low, grad_low):
    return jnp.einsum(
        "tf,td->fd", hidden_low, grad_low, preferred_element_type=jnp.float32
    ).astype(jnp.bfloat16)


def dense_back_out(grad_stream, stream, gain_row, weight_in, grad_pre):
    grad_normed = jnp.einsum("tf,df->td", grad_pre, weight_in, preferred_element_type=jnp.float32)
    grad_input, grad_gain = norm_backward(grad_normed, stream, gain_row)
    return (grad_stream + grad_input, grad_gain)


def dispatch_table(expert_ids, slot_ids, expert_count, capacity):
    target = jnp.where(slot_ids < capacity, expert_ids * capacity + slot_ids, -1)
    return (
        target[:, None] == jnp.arange(expert_count * capacity, dtype=jnp.int32)[None, :]
    ).astype(jnp.bfloat16)


def to_experts(slot_table, rows, experts_here):
    outgoing = jnp.einsum("ts,td->sd", slot_table, rows, preferred_element_type=F32).astype(BF16)
    expert_count = lax.axis_size(EXPERT_AXES) * experts_here
    capacity = rows.shape[0] // expert_count
    outgoing = outgoing.reshape(expert_count // experts_here, experts_here, capacity, -1)
    return lax.all_to_all(outgoing, EXPERT_AXES, split_axis=0, concat_axis=0, tiled=True)


def sparse_layer(
    stream, grad_stream, gain_row, router_full, in_full, out_experts, expert_ids, slot_ids
):
    normed_low = norm_scale(stream, gain_row.astype(F32)).astype(BF16)
    logits = jnp.dot(normed_low, router_full, preferred_element_type=F32)
    expert_count = router_full.shape[1]
    chosen = (expert_ids[:, None] == jnp.arange(expert_count, dtype=jnp.int32)[None, :]).astype(F32)
    gate_values = gate_of(logits, chosen)
    slot_table = dispatch_table(
        expert_ids, slot_ids, expert_count, stream.shape[0] // expert_count
    )
    grad_combined = (gate_values[:, None] * grad_stream).astype(BF16)
    received = to_experts(slot_table, normed_low, in_full.shape[0])
    grad_combined = after(grad_combined, received)
    grad_produced = to_experts(slot_table, grad_combined, in_full.shape[0])

    hidden_pre = jnp.einsum("secd,edf->secf", received, in_full, preferred_element_type=F32)
    gelu_value, gelu_pull = jax.vjp(gelu_tanh, hidden_pre)
    hidden_low = gelu_value.astype(BF16)
    produced = jnp.einsum(
        "secf,efd->secd", hidden_low, out_experts, preferred_element_type=F32
    ).astype(BF16)
    produced, grad_produced = together(produced, grad_produced)
    returned = lax.all_to_all(produced, EXPERT_AXES, split_axis=0, concat_axis=0, tiled=True)

    grad_hidden = (
        jnp.einsum("secd,efd->secf", grad_produced, out_experts, preferred_element_type=F32)
        .astype(BF16)
        .astype(F32)
    )
    grad_pre = gelu_pull(grad_hidden)[0].astype(BF16)
    grad_received = jnp.einsum(
        "secf,edf->secd", grad_pre, in_full, preferred_element_type=F32
    ).astype(BF16)
    returned, grad_received = together(returned, grad_received)
    grad_sent = lax.all_to_all(grad_received, EXPERT_AXES, split_axis=0, concat_axis=0, tiled=True)
    grad_w_out = jnp.einsum("secf,secd->efd", hidden_low, grad_produced, preferred_element_type=F32)

    combined = jnp.dot(
        slot_table, returned.reshape(slot_table.shape[1], -1), preferred_element_type=F32
    )
    stream_after = stream + gate_values[:, None] * combined
    grad_gates = jnp.sum(grad_stream * combined, axis=-1)
    gate_again, gate_pull = jax.vjp(gate_of, logits, chosen)
    grad_logits = gate_pull(grad_gates)[0].astype(BF16)
    grad_router = jnp.einsum("td,te->de", normed_low, grad_logits, preferred_element_type=F32)

    grad_sent, grad_w_out = together(grad_sent, grad_w_out.astype(BF16))
    grad_normed = jnp.dot(
        slot_table, grad_sent.reshape(slot_table.shape[1], -1), preferred_element_type=F32
    )
    grad_normed = grad_normed + jnp.einsum(
        "te,de->td", grad_logits, router_full, preferred_element_type=F32
    )
    grad_input, grad_gain = norm_backward(grad_normed, stream, gain_row)
    return (
        stream_after,
        grad_stream + grad_input,
        grad_gain,
        grad_router,
        (received, grad_pre),
        grad_w_out,
    )


def expert_weight_term(received, grad_pre):
    if received.shape[1] != 1:
        whole = jnp.einsum("secd,secf->edf", received, grad_pre, preferred_element_type=F32)
        return whole.astype(BF16)
    rows = received.reshape(-1, received.shape[-1])
    return weight_term(rows, grad_pre.reshape(-1, grad_pre.shape[-1]))[None]


def on_device(
    tokens_in,
    segment_ids,
    expert_index,
    expert_slot,
    attn_gain,
    qkv_weight,
    out_weight,
    rel_bias,
    ffn_gain,
    ffn_in,
    ffn_out,
    router,
    expert_in,
    expert_out,
    cotangent,
):
    width = tokens_in.shape[1]
    packed_width = qkv_weight.shape[2]
    expert_count = router.shape[1]
    small = jnp.concatenate([attn_gain.T, ffn_gain.T, router], axis=1)
    small_width = -(-small.shape[1] // 128) * 128
    small = jnp.pad(small, ((0, 0), (0, small_width - small.shape[1])))
    joined = packed_width + width
    hidden_width = ffn_in.shape[1]
    rows = ffn_in.shape[0]
    stack = ffn_out.shape[0] // rows
    first_shard = jnp.concatenate([qkv_weight[:, 0], out_weight[:, 0], small], axis=1)
    last_shard = jnp.concatenate([qkv_weight[:, 1], out_weight[:, 1]], axis=1)
    dense_shard = jnp.concatenate(
        [ffn_in] + [ffn_out[i * rows : (i + 1) * rows] for i in range(stack)], axis=1
    )
    first_line = gather_z(send_z(first_shard))
    first_across = send_across(first_line)
    rest_shard = jnp.concatenate([dense_shard, last_shard], axis=1)
    dense_width = dense_shard.shape[1]
    dense_line, last_line = gather_z(
        send_z(after(rest_shard, first_line), first_across[1]),
        (((0, dense_width),), ((dense_width, dense_width + last_shard.shape[1]),)),
    )
    bias = masked_bias(rel_bias, after(segment_ids, first_line))
    first_half = gather_across(first_across)
    first_half, dense_line, last_line, bias, expert_in, expert_out = together(
        first_half, dense_line, last_line, bias, expert_in, expert_out
    )
    in_full = lax.all_gather(expert_in, DATA_AXES, axis=1, tiled=True)
    out_experts = lax.all_gather(expert_out, DATA_AXES, axis=1, tiled=True)
    qkv_zero, out_zero, small_full = gather_core(
        first_half,
        (((0, packed_width),), ((packed_width, joined),), ((joined, joined + small_width),)),
    )
    gains = small_full[:, :4].T
    router_full = small_full[:, 4 : 4 + expert_count]

    stream_zero = tokens_in.astype(F32)
    attn_zero = attention_forward(stream_zero, gains[0], qkv_zero, out_zero, bias)
    dense_half = gather_across(send_around(dense_line, attn_zero[2]), attn_zero[2])
    ffn_in_full, ffn_out_full = gather_core(
        dense_half,
        (
            ((0, hidden_width),),
            tuple((hidden_width + i * width, hidden_width + (i + 1) * width) for i in range(stack)),
        ),
        attn_zero[4],
    )
    dense_zero = dense_forward(attn_zero[4], gains[2], ffn_in_full, ffn_out_full)
    last_half = gather_across(send_across(after(last_line, dense_half)), dense_zero[1])
    qkv_one, out_one = gather_core(
        last_half, (((0, packed_width),), ((packed_width, joined),)), dense_zero[2]
    )
    attn_one = attention_forward(dense_zero[2], gains[1], qkv_one, out_one, bias)
    (
        stream_two,
        grad_middle,
        ffn_gain_one,
        router_term,
        expert_in_rows,
        expert_out_term,
    ) = sparse_layer(
        attn_one[4],
        cotangent.astype(F32),
        gains[3],
        router_full,
        in_full,
        out_experts,
        expert_index,
        expert_slot,
    )
    expert_out_sum = lax.psum_scatter(
        expert_out_term, DATA_AXES, scatter_dimension=1, tiled=True
    )

    grad_mixed_one, out_one_term = attention_back_in(grad_middle, out_one, attn_one)
    packed_grad_one, pairs_one = attend_backward(attn_one[1], grad_mixed_one, attn_one[3])
    qkv_one_term = qkv_weight_term(packed_grad_one, attn_one)
    grad_one, attn_gain_one = attention_back_out(
        packed_grad_one, grad_middle, dense_zero[2], gains[1], qkv_one, attn_one
    )
    last_half = scatter_core([qkv_one_term, out_one_term])
    hidden_low, grad_low, grad_pre = dense_back_in(grad_one, ffn_out_full, dense_zero, last_half)
    last_terms = send_half(last_half)
    expert_in_term = expert_weight_term(*together(*expert_in_rows, grad_pre)[:2])
    expert_in_sum = lax.psum_scatter(
        expert_in_term, DATA_AXES, scatter_dimension=1, tiled=True
    )
    ffn_out_term = dense_out_term(hidden_low, grad_low)
    back_half = scatter_core([ffn_out_term])
    ffn_in_term = weight_term(dense_zero[0], grad_pre)
    back_half, grad_pre, last_terms, ffn_in_term = together(
        back_half, grad_pre, last_terms, ffn_in_term
    )
    back_terms = send_half(back_half)
    grad_half, ffn_gain_zero = dense_back_out(
        grad_one, attn_zero[4], gains[2], ffn_in_full, grad_pre
    )
    grad_mixed_zero, out_zero_term = attention_back_in(grad_half, out_zero, attn_zero)
    into_half = scatter_core([ffn_in_term])
    into_half, grad_mixed_zero = together(into_half, grad_mixed_zero)
    packed_grad_zero, pairs_zero = attend_backward(attn_zero[1], grad_mixed_zero, attn_zero[3])
    qkv_zero_term = qkv_weight_term(packed_grad_zero, attn_zero)
    first_half = scatter_core([qkv_zero_term, out_zero_term])
    into_half, back_terms, packed_grad_zero, pairs_zero = together(
        into_half, back_terms, packed_grad_zero, pairs_zero
    )
    into_terms = send_half(into_half)
    ffn_out_sum = sum_z(sum_half(back_terms))
    grad_zero, attn_gain_zero = attention_back_out(
        packed_grad_zero, grad_half, stream_zero, gains[0], qkv_zero, attn_zero
    )
    first_half, into_terms, ffn_out_sum, grad_zero, pairs_zero, last_terms = together(
        first_half, into_terms, ffn_out_sum, grad_zero, pairs_zero, last_terms
    )
    first_terms = send_half(first_half)
    tiny = jnp.concatenate(
        [
            attn_gain_zero,
            attn_gain_one,
            ffn_gain_zero,
            ffn_gain_one,
            router_term.reshape(-1),
            bias_grad(pairs_zero + pairs_one).reshape(-1),
        ]
    )
    tiny_sum = sum_along(tiny.reshape(-1, 128), ("core",))
    expert_in_sum, expert_out_sum, into_terms, last_terms = together(
        expert_in_sum, expert_out_sum, into_terms, last_terms
    )
    later_line = jnp.concatenate([sum_half(into_terms), sum_half(last_terms)], axis=-1)
    later_sum = sum_z(later_line)
    tiny_sum, first_terms, later_sum = together(tiny_sum, first_terms, later_sum)
    ffn_in_sum = later_sum[:, :hidden_width]
    one_sum = later_sum[:, hidden_width:]
    tiny_sum = sum_along(tiny_sum, (EXPERT_AXES, "z")).reshape(-1)
    zero_sum = sum_z(sum_half(first_terms))
    qkv_sum = jnp.stack([zero_sum[:, :packed_width], one_sum[:, :packed_width]], axis=1)
    out_sum = jnp.stack([zero_sum[:, packed_width:], one_sum[:, packed_width:]], axis=1)

    gain_sums = tiny_sum[: 4 * width].reshape(4, width)
    router_sums = tiny_sum[4 * width : (4 + expert_count) * width].reshape(width, expert_count)
    bias_sum = tiny_sum[(4 + expert_count) * width :].reshape(BUCKETS, HEADS)
    first_row = lax.axis_index(ALL_AXES) * rows
    gain_shard = lax.dynamic_slice_in_dim(gain_sums, first_row, rows, 1)
    router_shard = lax.dynamic_slice_in_dim(router_sums, first_row, rows, 0)
    return (
        stream_two.astype(BF16),
        grad_zero,
        gain_shard[:2],
        qkv_sum,
        out_sum,
        bias_sum,
        gain_shard[2:],
        ffn_in_sum,
        ffn_out_sum,
        router_shard,
        expert_in_sum.astype(F32),
        expert_out_sum.astype(F32),
    )


def solution(mesh):
    experts, data = mesh.shape["expert"], mesh.shape["dp"]
    side = 1 << ((experts.bit_length() - 1) // 2)
    fine = Mesh(mesh.devices.reshape(experts // side, side, data // 2, 2), ALL_AXES)
    placed = (
        P(ALL_AXES, None),
        P(ALL_AXES, None),
        P(ALL_AXES),
        P(ALL_AXES),
        P(None, ALL_AXES),
        P(ALL_AXES, None, None),
        P(ALL_AXES, None, None),
        P(),
        P(None, ALL_AXES),
        P(ALL_AXES, None),
        P(ALL_AXES, None),
        P(ALL_AXES, None),
        P(EXPERT_AXES, DATA_AXES, None),
        P(EXPERT_AXES, DATA_AXES, None),
        P(ALL_AXES, None),
    )
    return jax.shard_map(
        on_device,
        mesh=fine,
        in_specs=placed,
        out_specs=(
            P(ALL_AXES, None),
            P(ALL_AXES, None),
            P(None, ALL_AXES),
            P(ALL_AXES, None, None),
            P(ALL_AXES, None, None),
            P(),
            P(None, ALL_AXES),
            P(ALL_AXES, None),
            P(ALL_AXES, None),
            P(ALL_AXES, None),
            P(EXPERT_AXES, DATA_AXES, None),
            P(EXPERT_AXES, DATA_AXES, None),
        ),
        check_vma=False,
    )
```
